256 devices in a mesh: wide: 64 (over y, z, core), narrow: 4 (over x).
Axes of the slice: x: 4, y: 4, z: 8, core: 2. Of those that a mesh axis runs over, the one named last changes fastest.
Arguments:
- items: bfloat16 [131072, 256], P(('wide', 'narrow')), may hold values from -6 to 6
- tile1_values: bfloat16 [24576, 128, 128], P(('wide', 'narrow')), may hold values from -0.109375 to 0.109375
- tile1_source: int32 [24576], P(('wide', 'narrow')), may hold values from 0 to 3
- tile1_owner: int32 [24576, 1], P(('wide', 'narrow')), may hold values from 0 to 63; in each aligned block of 96 rows (0 to 95, 96 to 191, ...) at most 2 rows name the same one
- tile1_slot: int32 [24576], P(('wide', 'narrow')), may hold values from 0 to 3
- tile2_values: bfloat16 [24576, 128, 128], P(('wide', 'narrow')), may hold values from -0.109375 to 0.109375
- tile2_source: int32 [24576], P(('wide', 'narrow')), may hold values from 0 to 3
- tile2_owner: int32 [24576, 1], P(('wide', 'narrow')), may hold values from 0 to 63; in each aligned block of 96 rows (0 to 95, 96 to 191, ...) at most 2 rows name the same one
- tile2_slot: int32 [24576], P(('wide', 'narrow')), may hold values from 0 to 15
- weight: bfloat16 [256, 256], replicated, may hold values from -0.375 to 0.375
- bundle_degree: int32 [131072], P(('wide', 'narrow')), may hold values from 1 to 4
- user_degree: int32 [131072], P('wide'), may hold values from 1 to 4
- cotangent: bfloat16 [131072, 256], P('wide'), may hold values from -6 to 6
Outputs:
- user_out: bfloat16 [131072, 256], P('wide')
- grad_weight: float32 [256, 256], replicated
- grad_bundle: bfloat16 [131072, 256], P(('wide', 'narrow'))
The draws below stay inside these ranges and needn't reach their ends.
Inputs may be any that keep to these rules, and one draw needn't show every extreme that they name: `tile1_owner`: among the 96 tiles of one device, at most 2 name the same owner, a bound that some block reaches. `tile2_owner`: among the 96 tiles of one device, at most 2 name the same owner, a bound that some block reaches.
All inputs are finite; a program needn't handle non-finite values.
Results may differ from the reference program's by a relative error of at most 0.0073.
Values may be sent and summed in bfloat16 or wider, within the bound.
No kernel may reach another device: no remote copies, remote signals or barrier semaphores. Data moves between devices by JAX's collectives and lax.ppermute only.
A program may use at most 128 MiB of HBM per device.

```python
import math
import jax
import jax.numpy as jnp
import numpy as np
from jax import lax

F = 256
TILE = 128
CAP = 2
IB_DEV = 4
BB_DEV = 4
UGRP = 16
TILES1 = 96
TILES_ALL = 24576
ITEMS = 131072
BUNDLES = 131072
USERS = 131072
N_WIDE = 64
N_NARROW = 4
DEVICES = 256


def place_ends(result, rng, low, largest):
    index_at = [jax.random.randint(jax.random.fold_in(rng, axis), (), 0, length) for axis, length in enumerate(result.shape)]
    longest = result.shape.index(max(result.shape))
    next_to = index_at[:longest] + [(index_at[longest] + 1) % result.shape[longest]] + index_at[longest + 1:]
    return result.at[tuple(index_at)].set(low).at[tuple(next_to)].set(largest)


def block_levels(own_key, extent, cuts, least, largest):
    loudness = 1.0
    for axis_at, shards_of in cuts:
        draws = jax.random.uniform(jax.random.fold_in(jax.random.fold_in(own_key, 6), axis_at), (shards_of,), jnp.float32, least / len(cuts), largest / len(cuts))
        loudness = loudness * jnp.repeat(jnp.exp(draws), extent[axis_at] // shards_of).reshape((-1,) + (1,) * (len(extent) - 1 - axis_at))
    return loudness


def assign_block(rng, own, number, rows, amount, top, most, slope):
    order = jax.random.permutation(rng, amount)
    heavy_load, common = shares(amount, rows * top, most, slope, True), shares(amount, rows * top, most, slope, False)
    places = jnp.arange(amount)

    def named(sizes, rotation):
        used = int((sizes > 0).sum())
        fixed = max(1, used // 4)
        moved = fixed + (places - fixed + rotation * (used - fixed)) % max(1, amount - fixed)
        return jnp.zeros((amount,), jnp.int32).at[order[jnp.where(places < fixed, places, moved)]].set(jnp.asarray(sizes, jnp.int32))

    sizes = jnp.where(number % 4 == 0, named(heavy_load, number // 4), named(common, number - number // 4 - 1))
    mixed = jax.random.permutation(jax.random.fold_in(own, 3), amount)
    source_of, taker = mixed[0:amount // 2 * 2:2], mixed[1:amount // 2 * 2:2]
    slack = jnp.minimum(sizes[source_of] - 1, most - sizes[taker]) // 2
    slack = jnp.where((source_of == order[0]) | (taker == order[0]) | (sizes[taker] == 0), 0, jnp.maximum(slack, 0))
    moved = jax.random.randint(jax.random.fold_in(own, 4), (amount // 2,), 0, 1 << 20) % (slack + 1)
    sizes = sizes.at[source_of].add(-moved).at[taker].add(moved)
    labels = jnp.searchsorted(jnp.cumsum(sizes), jnp.arange(rows * top), side="right").astype(jnp.int32)
    listing = labels.reshape(top, rows).T
    listing = listing[jax.random.permutation(jax.random.fold_in(own, 1), rows)]
    rotation = jax.random.randint(jax.random.fold_in(own, 2), (rows, 1), 0, top)
    return jnp.take_along_axis(listing, (jnp.arange(top)[None, :] + rotation) % top, axis=1)


def shares(amount, total, most, skew, full):
    weights = [(1 << 20) // math.isqrt(standing ** skew) + 1 for standing in range(1, amount + 1)]
    largest = most if full else min(most, max(-(-total // amount), total * weights[0] // sum(weights)))
    least = 1 if total - largest >= amount - 1 else 0
    given, rest = [largest] + [least] * (amount - 1), total - largest - least * (amount - 1)
    while rest > 0:
        free = [i for i in range(1, amount) if given[i] < largest] or [i for i in range(1, amount) if given[i] < most]
        pool, remaining = sum([weights[i] for i in free]), rest
        for i in free:
            addition = min(most - given[i], max(1, remaining * weights[i] // pool), rest)
            given[i] = given[i] + addition
            rest = rest - addition
    return np.array(given)


def normal_values(key, dims, scale, reach, split=(), kind=jnp.bfloat16):
    entries = jax.random.normal(key, dims, jnp.float32) * scale
    if len(split) > 0:
        entries = block_levels(key, dims, split, -0.22, 0.18) * entries
    return jnp.clip(entries, min=-reach, max=reach).astype(kind)


def setup_inputs(seed: int = 0) -> dict:
    splits = jax.random.split(jax.random.key(seed), 14)
    items = normal_values(splits[0], (ITEMS, F), 1.0, 6.0, ((0, 256),))
    tile1_values = normal_values(splits[1], (TILES_ALL, TILE, TILE), (TILE * TILES1 // BB_DEV) ** -0.5, 0.109375, ((0, 256),))
    tile1_source = place_ends(jax.random.randint(splits[2], (TILES_ALL,), 0, IB_DEV), jax.random.fold_in(splits[2], 1), 0, IB_DEV - 1).astype(jnp.int32)
    tile1_owner_keys = jax.random.split(jax.random.fold_in(splits[3], 1), TILES_ALL // TILES1)
    tile1_owner_turns = jax.random.permutation(jax.random.fold_in(splits[3], 3), TILES_ALL // TILES1)
    tile1_owner = jax.vmap(lambda own, number: assign_block(jax.random.fold_in(splits[3], 2), own, number, TILES1, N_WIDE, 1, CAP, 2))(tile1_owner_keys, tile1_owner_turns).reshape((TILES_ALL, 1))
    tile1_slot = place_ends(jax.random.randint(splits[4], (TILES_ALL,), 0, BB_DEV), jax.random.fold_in(splits[4], 1), 0, BB_DEV - 1).astype(jnp.int32)
    tile2_values = normal_values(splits[5], (TILES_ALL, TILE, TILE), (TILE * TILES1 * N_NARROW // UGRP) ** -0.5, 0.109375, ((0, 256),))
    tile2_source = place_ends(jax.random.randint(splits[6], (TILES_ALL,), 0, BB_DEV), jax.random.fold_in(splits[6], 1), 0, BB_DEV - 1).astype(jnp.int32)
    tile2_owner_keys = jax.random.split(jax.random.fold_in(splits[7], 1), TILES_ALL // TILES1)
    tile2_owner_turns = jax.random.permutation(jax.random.fold_in(splits[7], 3), TILES_ALL // TILES1)
    tile2_owner = jax.vmap(lambda own, number: assign_block(jax.random.fold_in(splits[7], 2), own, number, TILES1, N_WIDE, 1, CAP, 2))(tile2_owner_keys, tile2_owner_turns).reshape((TILES_ALL, 1))
    tile2_slot = place_ends(jax.random.randint(splits[8], (TILES_ALL,), 0, UGRP), jax.random.fold_in(splits[8], 1), 0, UGRP - 1).astype(jnp.int32)
    weight = normal_values(splits[9], (F, F), F ** -0.5, 0.375)
    bundle_degree = place_ends(jax.random.randint(splits[10], (BUNDLES,), 1, 5), jax.random.fold_in(splits[10], 1), 1, 4).astype(jnp.int32)
    user_degree = place_ends(jax.random.randint(splits[11], (USERS,), 1, 5), jax.random.fold_in(splits[11], 1), 1, 4).astype(jnp.int32)
    cotangent = normal_values(splits[12], (USERS, F), 1.0, 6.0, ((0, 64),))
    return dict(items=items, tile1_values=tile1_values, tile1_source=tile1_source, tile1_owner=tile1_owner, tile1_slot=tile1_slot, tile2_values=tile2_values, tile2_source=tile2_source, tile2_owner=tile2_owner, tile2_slot=tile2_slot, weight=weight, bundle_degree=bundle_degree, user_degree=user_degree, cotangent=cotangent)


def spread(values, blocks, take, put, count, flip):
    vals = values.reshape(DEVICES, TILES1, TILE, TILE)
    take = take.reshape(DEVICES, TILES1).astype(jnp.int32)
    put = put.reshape(DEVICES, TILES1).astype(jnp.int32)
    form = "tji,tjf->tif" if flip else "tij,tjf->tif"

    def step(acc, inputs):
        tiles, taken, placed = inputs
        source = blocks[taken].astype(jnp.float32)
        product = jnp.einsum(form, tiles.astype(jnp.float32), source)
        product = lax.optimization_barrier(product.astype(jnp.bfloat16)).astype(jnp.float32)
        return acc.at[placed].add(product), None

    acc, _ = lax.scan(step, jnp.zeros((count, TILE, F), jnp.float32), (vals, take, put))
    return acc.reshape(count * TILE, F)


def reference(items, tile1_values, tile1_source, tile1_owner, tile1_slot, tile2_values, tile2_source, tile2_owner, tile2_slot, weight, bundle_degree, user_degree, cotangent):
    device = jnp.arange(TILES_ALL, dtype=jnp.int32) // TILES1
    narrow_of = device % N_NARROW
    source1 = device * IB_DEV + tile1_source
    target1 = (tile1_owner[:, 0] * N_NARROW + narrow_of) * BB_DEV + tile1_slot
    summed = spread(tile1_values, items.reshape(-1, TILE, F), source1, target1, BUNDLES // TILE, False)
    bundle_emb = (summed / bundle_degree[:, None].astype(jnp.float32)).astype(jnp.bfloat16)
    mixed = jnp.dot(bundle_emb, weight, preferred_element_type=jnp.float32)
    activated = jax.nn.silu(mixed).astype(jnp.bfloat16)
    source2 = device * BB_DEV + tile2_source
    target2 = tile2_owner[:, 0] * UGRP + tile2_slot
    gathered = spread(tile2_values, activated.reshape(-1, TILE, F), source2, target2, USERS // TILE, False)
    user_out = (gathered / user_degree[:, None].astype(jnp.float32)).astype(jnp.bfloat16)
    scaled_grad = (cotangent.astype(jnp.float32) / user_degree[:, None].astype(jnp.float32)).astype(jnp.bfloat16)
    grad_act = spread(tile2_values, scaled_grad.reshape(-1, TILE, F), target2, source2, BUNDLES // TILE, True)
    sigma = jax.nn.sigmoid(mixed)
    grad_mixed = (grad_act * sigma * (1.0 + mixed * (1.0 - sigma))).astype(jnp.bfloat16)
    grad_weight = jnp.dot(bundle_emb.T, grad_mixed, preferred_element_type=jnp.float32)
    grad_bundle = jnp.dot(grad_mixed, weight.T, preferred_element_type=jnp.float32).astype(jnp.bfloat16)
    return user_out, grad_weight, grad_bundle
```

```python
import jax
import jax.numpy as jnp
from jax import lax
from jax.experimental import pallas as pl
from jax.experimental.pallas import tpu as pltpu
from jax.sharding import Mesh, PartitionSpec as P

F = 256
TILE = 128
TILES = 96
BLK = 4
UGRP = 16
NY, NZ, NC, NX = 4, 8, 2, 4
WIDE = ("y", "z", "c")
ALL = ("y", "z", "c", "x")
LAB = 16
BF16 = jnp.bfloat16
F32 = jnp.float32
VMEM_LIMIT = 48 * 1024 * 1024

SMEM_SPEC = pl.BlockSpec(memory_space=pltpu.SMEM)
VMEM_SPEC = pl.BlockSpec(memory_space=pltpu.VMEM)
ANY_SPEC = pl.BlockSpec(memory_space=pl.ANY)


def pack(me, first, second):
    parts = (first, second)
    shapes = [(p["groups"], p["cap"] * TILE + LAB, TILE) for p in parts]

    def kernel(me_ref, *rest):
        refs = (rest[0:4], rest[4:8])
        groups1 = shapes[0][0]
        outs1, out2 = rest[8 : 8 + groups1], rest[8 + groups1]
        tiles1, tiles2, room1, room2, count, labels, in_sems, sems1, sem2 = rest[9 + groups1 :]
        loads = [
            pltpu.make_async_copy(refs[1][3], tiles2, in_sems.at[1]),
            pltpu.make_async_copy(refs[0][3], tiles1, in_sems.at[0]),
        ]
        for load in loads:
            load.start()
        lane = lax.broadcasted_iota(jnp.int32, (1, TILE), 1)

        def lay(part, part_refs, tiles_ref, room):
            source_ref, owner_ref, slot_ref = part_refs[:3]
            groups, rows, _ = room.shape
            for g in range(groups):
                count[g] = 0
            labels[...] = jnp.full(labels.shape, float(BLK * part["dummy"]), F32)

            def step(t, carry):
                own = owner_ref[t]
                g = part["group_of"](own, me_ref)
                rank = count[g]
                count[g] = rank + 1
                row = pl.multiple_of(rank * TILE, TILE)
                room[g, pl.ds(row, TILE), :] = tiles_ref[t]
                label = (BLK * part["block_of"](own, slot_ref[t]) + source_ref[t]).astype(F32)
                old = labels[pl.ds(g, 1), :]
                labels[pl.ds(g, 1), :] = jnp.where(lane == rank, label, old)
                return carry

            lax.fori_loop(0, TILES, step, 0)
            room[:, rows - LAB : rows, :] = jnp.broadcast_to(
                labels[0:groups][:, None, :], (groups, LAB, TILE)
            ).astype(BF16)

        loads[0].wait()
        lay(second, refs[1], tiles2, room2)
        copies = [pltpu.make_async_copy(room2, out2, sem2)]
        copies[0].start()
        loads[1].wait()
        lay(first, refs[0], tiles1, room1)
        for g in range(groups1):
            copies.append(pltpu.make_async_copy(room1.at[g], outs1[g], sems1.at[g]))
            copies[-1].start()
        for copy in copies:
            copy.wait()

    out_shape = [jax.ShapeDtypeStruct(shapes[0][1:], BF16)] * shapes[0][0]
    out_shape.append(jax.ShapeDtypeStruct(shapes[1], BF16))
    most = max(shapes[0][0], shapes[1][0])
    outs = pl.pallas_call(
        kernel,
        out_shape=out_shape,
        in_specs=[SMEM_SPEC] + [SMEM_SPEC, SMEM_SPEC, SMEM_SPEC, ANY_SPEC] * 2,
        out_specs=[ANY_SPEC] * len(out_shape),
        scratch_shapes=[
            pltpu.VMEM((TILES, TILE, TILE), BF16),
            pltpu.VMEM((TILES, TILE, TILE), BF16),
            pltpu.VMEM(shapes[0], BF16),
            pltpu.VMEM(shapes[1], BF16),
            pltpu.SMEM((most,), jnp.int32),
            pltpu.VMEM((most, TILE), F32),
            pltpu.SemaphoreType.DMA((2,)),
            pltpu.SemaphoreType.DMA((shapes[0][0],)),
            pltpu.SemaphoreType.DMA,
        ],
        compiler_params=pltpu.CompilerParams(vmem_limit_bytes=VMEM_LIMIT),
        cost_estimate=pl.CostEstimate(flops=0, bytes_accessed=16 * 1024 * 1024, transcendentals=0),
        name="pack",
    )(me, *first["args"], *second["args"])
    return outs[:-1], outs[-1]


def labels_of(received, cap):
    return received[..., cap * TILE, :cap].astype(jnp.int32)


def products(labels, bases, received, blocks, cap, count, split_out, flip):
    groups = len(received) if isinstance(received, (list, tuple)) else received.shape[0]
    many = isinstance(received, (list, tuple))
    tiles_in = list(received) if many else [received]
    n_out = (split_out > 0) + (split_out < count)

    def kernel(lab_ref, base_ref, *rest):
        tile_refs, blocks_ref = rest[: len(tiles_in)], rest[len(tiles_in)]
        outs, acc = rest[len(tiles_in) + 1 : -1], rest[-1]
        acc[...] = jnp.zeros_like(acc)

        def one(i, g, tile):
            lab = lab_ref[i]
            near = base_ref[g] + lax.rem(lab, BLK)
            far = lax.div(lab, BLK)
            if flip:
                empty = far >= blocks.shape[0]
                into = jnp.where(empty, count, near)
                block = blocks_ref[jnp.where(empty, 0, far)]
                term = lax.dot_general(tile, block, (((0,), (0,)), ((), ())), preferred_element_type=F32)
            else:
                into = far
                term = jnp.dot(tile, blocks_ref[near], preferred_element_type=F32)
            acc[into] = acc[into] + term

        if many:
            for g, ref in enumerate(tile_refs):

                def step(k, carry, g=g, ref=ref):
                    row = pl.multiple_of(k * TILE, TILE)
                    one(g * cap + k, g, ref[pl.ds(row, TILE), :])
                    return carry

                lax.fori_loop(0, cap, step, 0, unroll=4)
        else:

            def step(i, carry):
                row = pl.multiple_of((i % cap) * TILE, TILE)
                one(i, i // cap, tile_refs[0][i // cap, pl.ds(row, TILE), :])
                return carry

            lax.fori_loop(0, groups * cap, step, 0, unroll=4)
        at = 0
        if split_out > 0:
            outs[at][...] = acc[0:split_out]
            at += 1
        if split_out < count:
            outs[at][...] = acc[split_out:count].astype(BF16)

    out_shape = []
    if split_out > 0:
        out_shape.append(jax.ShapeDtypeStruct((split_out, TILE, F), F32))
    if split_out < count:
        out_shape.append(jax.ShapeDtypeStruct((count - split_out, TILE, F), BF16))
    return pl.pallas_call(
        kernel,
        out_shape=out_shape,
        in_specs=[SMEM_SPEC, SMEM_SPEC] + [VMEM_SPEC] * (len(tiles_in) + 1),
        out_specs=[VMEM_SPEC] * n_out,
        scratch_shapes=[pltpu.VMEM((count + 1, TILE, F), F32)],
        compiler_params=pltpu.CompilerParams(vmem_limit_bytes=VMEM_LIMIT),
        cost_estimate=pl.CostEstimate(
            flops=2 * groups * cap * TILE * TILE * F, bytes_accessed=12 * 1024 * 1024, transcendentals=0
        ),
        name="back_products" if flip else "products",
    )(labels, bases, *tiles_in, blocks)


def all_to_all(value, axes):
    return lax.all_to_all(value, axes, split_axis=0, concat_axis=0, tiled=True)


def local(
    items,
    tile1_values,
    tile1_source,
    tile1_owner,
    tile1_slot,
    tile2_values,
    tile2_source,
    tile2_owner,
    tile2_slot,
    weight,
    bundle_degree,
    user_degree,
    cotangent,
):
    y, z, c, x = (lax.axis_index(a) for a in ALL)
    me = jnp.stack([y, c]).astype(jnp.int32)
    near1, near2 = NY * NC, NZ * NC
    cap1, cap2 = TILE // near1, TILE // near2

    def group1(own, me_ref):
        dest_y, dest_c = own // (NZ * NC), own % NC
        return ((dest_y - me_ref[0] + NY) % NY) * NC + (dest_c - me_ref[1] + NC) % NC

    send1, send2 = pack(
        me,
        dict(
            args=(tile1_source, tile1_owner[:, 0], tile1_slot, tile1_values),
            groups=near1, cap=cap1, group_of=group1, dummy=NZ * BLK,
            block_of=lambda own, slot: ((own // NC) % NZ) * BLK + slot,
        ),
        dict(
            args=(tile2_source, tile2_owner[:, 0], tile2_slot, tile2_values),
            groups=near2, cap=cap2, group_of=lambda own, me_ref: own % (NZ * NC), dummy=NY * UGRP,
            block_of=lambda own, slot: (own // (NZ * NC)) * UGRP + slot,
        ),
    )
    senders = jnp.arange(near1, dtype=jnp.int32)
    got1 = [send1[0]]
    for offset in range(1, near1):
        pairs = [
            (a * NC + b, ((a + offset // NC) % NY) * NC + (b + offset) % NC)
            for a in range(NY) for b in range(NC)
        ]
        got1.append(lax.ppermute(send1[offset], ("y", "c"), pairs))
    labels1 = jnp.concatenate([labels_of(part, cap1) for part in got1])
    bases1 = (((y - senders // NC + NY) % NY) * NC + (c + senders) % NC) * BLK
    got2 = all_to_all(send2, ("z", "c"))
    near_items = lax.all_gather(items, ("y", "c"), axis=0, tiled=True)

    rows = user_degree.shape[0] // NX
    degree = lax.dynamic_slice_in_dim(user_degree, x * rows, rows)[:, None].astype(F32)
    cot = lax.dynamic_slice_in_dim(cotangent, x * rows, rows)
    scaled_grad = (cot.astype(F32) / degree).astype(BF16)
    got2, scaled_grad = lax.optimization_barrier((got2, scaled_grad))
    near_grad = all_to_all(jnp.broadcast_to(scaled_grad, (NY * NX, rows, F)), ("y", "x"))

    part1 = products(
        labels1, bases1, got1, near_items.reshape(-1, TILE, F), cap1, NZ * BLK, NZ * BLK, False
    )[0]
    got2, part1 = lax.optimization_barrier((got2, part1))
    summed = lax.psum_scatter(part1.reshape(-1, F), "z", scatter_dimension=0, tiled=True)
    summed, near_grad = lax.optimization_barrier((summed, near_grad))
    bundle_emb = (summed / bundle_degree[:, None].astype(F32)).astype(BF16)
    mixed = jnp.dot(bundle_emb, weight, preferred_element_type=F32)
    activated = jax.nn.silu(mixed).astype(BF16)
    near_act = lax.all_gather(activated, ("z", "c"), axis=0, tiled=True)

    labels2 = labels_of(got2, cap2).reshape(-1)
    senders = jnp.arange(near2, dtype=jnp.int32)
    halves = ((senders + c) % NC) * (NZ * BLK) + (senders // NC) * BLK
    mine, other = products(
        labels2, halves, got2, near_grad.reshape(-1, TILE, F), cap2, NC * NZ * BLK, NZ * BLK, True
    )
    other = lax.ppermute(other, "c", [(0, 1), (1, 0)])
    both = (mine + other.astype(F32)).reshape(-1, F)
    near_act, both = lax.optimization_barrier((near_act, both))
    grad_act = lax.psum_scatter(both, "z", scatter_dimension=0, tiled=True)
    sigma = jax.nn.sigmoid(mixed)
    grad_mixed = (grad_act * sigma * (1.0 + mixed * (1.0 - sigma))).astype(BF16)
    local_grad = lax.dot_general(
        bundle_emb, grad_mixed, (((0,), (0,)), ((), ())), preferred_element_type=F32
    )
    grad_bundle = lax.dot_general(
        grad_mixed, weight, (((1,), (1,)), ((), ())), preferred_element_type=F32
    ).astype(BF16)

    part2 = products(
        labels2, senders * BLK, got2, near_act.reshape(-1, TILE, F), cap2, NY * UGRP, 0, False
    )[0]
    got_part = all_to_all(part2.reshape(NY * NX, rows, F), ("y", "x"))
    gathered = jnp.sum(got_part.astype(F32), axis=0)
    user_part = (gathered / degree).astype(BF16)
    user_out = lax.all_gather(user_part, "x", axis=0, tiled=True)

    piece = jnp.sum(all_to_all(local_grad.reshape(near2, -1, F), ("z", "c")), axis=0)
    piece = jnp.sum(all_to_all(jnp.broadcast_to(piece, (NY * NX,) + piece.shape), ("y", "x")), axis=0)
    grad_weight = all_to_all(jnp.broadcast_to(piece, (near2,) + piece.shape), ("z", "c")).reshape(F, F)
    return (user_out, grad_weight, grad_bundle)


def solution(mesh):
    axes = Mesh(mesh.devices.reshape(NY, NZ, NC, NX), ALL)
    in_specs = (
        P(ALL, None),
        P(ALL, None, None),
        P(ALL),
        P(ALL, None),
        P(ALL),
        P(ALL, None, None),
        P(ALL),
        P(ALL, None),
        P(ALL),
        P(),
        P(ALL),
        P(WIDE),
        P(WIDE, None),
    )
    out_specs = (P(WIDE, None), P(), P(ALL, None))
    return jax.shard_map(local, mesh=axes, in_specs=in_specs, out_specs=out_specs, check_vma=False)
```

```python
import jax
import jax.numpy as jnp
from jax import lax
from jax.experimental import pallas as pl
from jax.experimental.pallas import tpu as pltpu
from jax.sharding import Mesh, PartitionSpec as P

F = 256
TILE = 128
TILES = 96
BLK = 4
UGRP = 16
NY, NZ, NC, NX = 4, 8, 2, 4
WIDE = ("y", "z", "c")
ALL = ("y", "z", "c", "x")
LAB = 16
BF16 = jnp.bfloat16
F32 = jnp.float32
VMEM_LIMIT = 48 * 1024 * 1024

SMEM_SPEC = pl.BlockSpec(memory_space=pltpu.SMEM)
VMEM_SPEC = pl.BlockSpec(memory_space=pltpu.VMEM)
ANY_SPEC = pl.BlockSpec(memory_space=pl.ANY)


def pack(me, first, second):
    parts = (first, second)
    shapes = [(p["groups"], p["cap"] * TILE + LAB, TILE) for p in parts]

    def kernel(me_ref, *rest):
        given = (rest[0:4], rest[4:8])
        groups1 = shapes[0][0]
        outs1, out2 = rest[8 : 8 + groups1], rest[8 + groups1]
        tiles1, tiles2, room1, room2, count, labels, in_sems, sems1, sem2 = rest[9 + groups1 : 18 + groups1]
        indices = rest[18 + groups1 : 24 + groups1]
        refs = (indices[0:3], indices[3:6])
        small = [
            pltpu.make_async_copy(given[i // 3][i % 3], indices[i], in_sems.at[2 + i]) for i in range(6)
        ]
        loads = [
            pltpu.make_async_copy(given[1][3], tiles2, in_sems.at[1]),
            pltpu.make_async_copy(given[0][3], tiles1, in_sems.at[0]),
        ]
        for load in small + loads:
            load.start()
        lane = lax.broadcasted_iota(jnp.int32, (1, TILE), 1)

        def lay(part, part_refs, tiles_ref, room):
            source_ref, owner_ref, slot_ref = part_refs[:3]
            groups, rows, _ = room.shape
            for g in range(groups):
                count[g] = 0
            labels[...] = jnp.full(labels.shape, float(BLK * part["dummy"]), F32)

            def step(t, carry):
                own = owner_ref[t]
                g = part["group_of"](own, me_ref)
                rank = count[g]
                count[g] = rank + 1
                row = pl.multiple_of(rank * TILE, TILE)
                room[g, pl.ds(row, TILE), :] = tiles_ref[t]
                label = (BLK * part["block_of"](own, slot_ref[t], me_ref) + source_ref[t]).astype(F32)
                old = labels[pl.ds(g, 1), :]
                labels[pl.ds(g, 1), :] = jnp.where(lane == rank, label, old)
                return carry

            lax.fori_loop(0, TILES, step, 0)
            room[:, rows - LAB : rows, :] = jnp.broadcast_to(
                labels[0:groups][:, None, :], (groups, LAB, TILE)
            ).astype(BF16)

        for load in small:
            load.wait()
        loads[0].wait()
        lay(second, refs[1], tiles2, room2)
        copies = [pltpu.make_async_copy(room2, out2, sem2)]
        copies[0].start()
        loads[1].wait()
        lay(first, refs[0], tiles1, room1)
        for g in range(groups1):
            copies.append(pltpu.make_async_copy(room1.at[g], outs1[g], sems1.at[g]))
            copies[-1].start()
        for copy in copies:
            copy.wait()

    out_shape = [jax.ShapeDtypeStruct(shapes[0][1:], BF16)] * shapes[0][0]
    out_shape.append(jax.ShapeDtypeStruct(shapes[1], BF16))
    most = max(shapes[0][0], shapes[1][0])
    outs = pl.pallas_call(
        kernel,
        out_shape=out_shape,
        in_specs=[SMEM_SPEC] + [ANY_SPEC] * 8,
        out_specs=[ANY_SPEC] * len(out_shape),
        scratch_shapes=[
            pltpu.VMEM((TILES, TILE, TILE), BF16),
            pltpu.VMEM((TILES, TILE, TILE), BF16),
            pltpu.VMEM(shapes[0], BF16),
            pltpu.VMEM(shapes[1], BF16),
            pltpu.SMEM((most,), jnp.int32),
            pltpu.VMEM((most, TILE), F32),
            pltpu.SemaphoreType.DMA((8,)),
            pltpu.SemaphoreType.DMA((shapes[0][0],)),
            pltpu.SemaphoreType.DMA,
        ]
        + [pltpu.SMEM((TILES,), jnp.int32)] * 6,
        compiler_params=pltpu.CompilerParams(vmem_limit_bytes=VMEM_LIMIT),
        cost_estimate=pl.CostEstimate(flops=0, bytes_accessed=16 * 1024 * 1024, transcendentals=0),
        name="pack",
    )(me, *first["args"], *second["args"])
    return outs[:-1], outs[-1]


def labels_of(received, cap):
    return received[..., cap * TILE, :cap].astype(jnp.int32)


def products(labels, bases, received, blocks, places, cap, count, split_out, flip):
    many = isinstance(received, (list, tuple))
    tiles_in = list(received) if many else [received]
    groups = len(received) if many else received.shape[0]
    n_out = (split_out > 0) + (split_out < count)
    n_in, n_blocks = len(tiles_in), len(blocks)
    blocks = [b.reshape(-1, TILE, F) for b in blocks]
    total = sum(b.shape[0] for b in blocks)

    def kernel(lab_ref, base_ref, place_ref, *rest):
        tile_refs, block_refs = rest[:n_in], rest[n_in : n_in + n_blocks]
        outs = rest[n_in + n_blocks : n_in + n_blocks + n_out]
        acc, room, tiles, sems, tile_sems = rest[n_in + n_blocks + n_out :]
        loads = [
            pltpu.make_async_copy(ref, room.at[pl.ds(place_ref[i], blocks[i].shape[0])], sems.at[i])
            for i, ref in enumerate(block_refs)
        ]
        rows = cap * TILE
        tile_loads = []
        for g in range(groups):
            source = tile_refs[g].at[pl.ds(0, rows), :] if many else tile_refs[0].at[g, pl.ds(0, rows), :]
            tile_loads.append(pltpu.make_async_copy(source, tiles.at[g], tile_sems.at[g]))
        for load in loads + tile_loads:
            load.start()
        acc[...] = jnp.zeros_like(acc)
        for load in loads:
            load.wait()

        def one(i, g, tile):
            lab = lab_ref[i]
            near = base_ref[g] + lax.rem(lab, BLK)
            far = lax.div(lab, BLK)
            if flip:
                empty = far >= total
                into = jnp.where(empty, count, near)
                block = room[jnp.where(empty, 0, far)]
                term = lax.dot_general(tile, block, (((0,), (0,)), ((), ())), preferred_element_type=F32)
            else:
                into = far
                term = jnp.dot(tile, room[near], preferred_element_type=F32)
            acc[into] = acc[into] + term

        for g in range(groups):

            def step(k, carry, g=g):
                row = pl.multiple_of(k * TILE, TILE)
                one(g * cap + k, g, tiles[g, pl.ds(row, TILE), :])
                return carry

            tile_loads[g].wait()
            lax.fori_loop(0, cap, step, 0, unroll=4)
        at = 0
        if split_out > 0:
            outs[at][...] = acc[0:split_out]
            at += 1
        if split_out < count:
            outs[at][...] = acc[split_out:count].astype(BF16)

    out_shape = []
    if split_out > 0:
        out_shape.append(jax.ShapeDtypeStruct((split_out, TILE, F), F32))
    if split_out < count:
        out_shape.append(jax.ShapeDtypeStruct((count - split_out, TILE, F), BF16))
    return pl.pallas_call(
        kernel,
        out_shape=out_shape,
        in_specs=[SMEM_SPEC, SMEM_SPEC, SMEM_SPEC] + [ANY_SPEC] * (n_in + n_blocks),
        out_specs=[VMEM_SPEC] * n_out,
        scratch_shapes=[
            pltpu.VMEM((count + 1, TILE, F), F32),
            pltpu.VMEM((total, TILE, F), BF16),
            pltpu.VMEM((groups, cap * TILE, TILE), BF16),
            pltpu.SemaphoreType.DMA((n_blocks,)),
            pltpu.SemaphoreType.DMA((groups,)),
        ],
        compiler_params=pltpu.CompilerParams(vmem_limit_bytes=VMEM_LIMIT),
        cost_estimate=pl.CostEstimate(
            flops=2 * groups * cap * TILE * TILE * F, bytes_accessed=12 * 1024 * 1024, transcendentals=0
        ),
        name="back_products" if flip else "products",
    )(labels, bases, places, *tiles_in, *blocks)


def all_to_all(value, axes):
    return lax.all_to_all(value, axes, split_axis=0, concat_axis=0, tiled=True)


def local(
    items,
    tile1_values,
    tile1_source,
    tile1_owner,
    tile1_slot,
    tile2_values,
    tile2_source,
    tile2_owner,
    tile2_slot,
    weight,
    bundle_degree,
    user_degree,
    cotangent,
):
    y, z, c, x = (lax.axis_index(a) for a in ALL)
    me = jnp.stack([y, c]).astype(jnp.int32)
    near1, near2 = NY, NZ * NC
    cap1, cap2 = TILE // near1, TILE // near2
    both1 = NC * NZ * BLK
    send1, send2 = pack(
        me,
        dict(
            args=(tile1_source, tile1_owner[:, 0], tile1_slot, tile1_values),
            groups=near1, cap=cap1, dummy=both1,
            group_of=lambda own, me_ref: (own // (NZ * NC) - me_ref[0] + NY) % NY,
            block_of=lambda own, slot, me_ref: (((own + me_ref[1]) % NC) * NZ + (own // NC) % NZ) * BLK + slot,
        ),
        dict(
            args=(tile2_source, tile2_owner[:, 0], tile2_slot, tile2_values),
            groups=near2, cap=cap2, dummy=NY * UGRP,
            group_of=lambda own, me_ref: own % (NZ * NC),
            block_of=lambda own, slot, me_ref: (own // (NZ * NC)) * UGRP + slot,
        ),
    )
    got1, near_items = [send1[0]], [items]
    for dy in range(1, NY):
        pairs = [(a, (a + dy) % NY) for a in range(NY)]
        near_items.append(lax.ppermute(items, "y", pairs))
        got1.append(lax.ppermute(send1[dy], "y", pairs))
    labels1 = jnp.concatenate([labels_of(part, cap1) for part in got1])
    places1 = jnp.arange(NY, dtype=jnp.int32) * BLK
    got2 = all_to_all(send2, ("z", "c"))
    rows = user_degree.shape[0] // NX
    degree = lax.dynamic_slice_in_dim(user_degree, x * rows, rows)[:, None].astype(F32)
    zero = jnp.zeros((1,), jnp.int32)
    cot = lax.dynamic_slice_in_dim(cotangent, x * rows, rows)
    scaled_grad = (cot.astype(F32) / degree).astype(BF16)
    near_grad = lax.all_gather(scaled_grad, ("y", "x"), axis=0, tiled=True)

    near_grad, labels1 = lax.optimization_barrier((near_grad, labels1))
    mine, other = products(labels1, places1, got1, near_items, places1, cap1, both1, both1 // NC, False)
    other = lax.ppermute(other, "c", [(0, 1), (1, 0)])
    part1 = (mine + other.astype(F32)).reshape(-1, F)
    got2, part1 = lax.optimization_barrier((got2, part1))
    summed = lax.psum_scatter(part1, "z", scatter_dimension=0, tiled=True)
    bundle_emb = (summed / bundle_degree[:, None].astype(F32)).astype(BF16)
    mixed = jnp.dot(bundle_emb, weight, preferred_element_type=F32)
    activated = jax.nn.silu(mixed).astype(BF16)
    near_act = lax.all_gather(activated, ("z", "c"), axis=0, tiled=True)

    labels2 = labels_of(got2, cap2).reshape(-1)
    senders = jnp.arange(near2, dtype=jnp.int32)
    halves = ((senders + c) % NC) * (NZ * BLK) + (senders // NC) * BLK
    mine, other = products(
        labels2, halves, got2, [near_grad], zero, cap2, NC * NZ * BLK, NZ * BLK, True
    )
    other = lax.ppermute(other, "c", [(0, 1), (1, 0)])
    both = (mine + other.astype(F32)).reshape(-1, F)
    near_act, both = lax.optimization_barrier((near_act, both))
    grad_act = lax.psum_scatter(both, "z", scatter_dimension=0, tiled=True)
    sigma = jax.nn.sigmoid(mixed)
    grad_mixed = (grad_act * sigma * (1.0 + mixed * (1.0 - sigma))).astype(BF16)
    local_grad = lax.dot_general(
        bundle_emb, grad_mixed, (((0,), (0,)), ((), ())), preferred_element_type=F32
    )
    grad_bundle = lax.dot_general(
        grad_mixed, weight, (((1,), (1,)), ((), ())), preferred_element_type=F32
    ).astype(BF16)

    part2 = products(
        labels2, senders * BLK, got2, [near_act], zero, cap2, NY * UGRP, 0, False
    )[0]
    got_part = all_to_all(part2.reshape(NY * NX, rows, F), ("y", "x"))
    gathered = jnp.sum(got_part.astype(F32), axis=0)
    user_part = (gathered / degree).astype(BF16)
    user_out = lax.all_gather(user_part, "x", axis=0, tiled=True)

    piece = jnp.sum(all_to_all(local_grad.reshape(near2, -1, F), ("z", "c")), axis=0)
    piece = jnp.sum(all_to_all(jnp.broadcast_to(piece, (NY * NX,) + piece.shape), ("y", "x")), axis=0)
    grad_weight = all_to_all(jnp.broadcast_to(piece, (near2,) + piece.shape), ("z", "c")).reshape(F, F)
    return (user_out, grad_weight, grad_bundle)


def solution(mesh):
    axes = Mesh(mesh.devices.reshape(NY, NZ, NC, NX), ALL)
    in_specs = (
        P(ALL, None),
        P(ALL, None, None),
        P(ALL),
        P(ALL, None),
        P(ALL),
        P(ALL, None, None),
        P(ALL),
        P(ALL, None),
        P(ALL),
        P(),
        P(ALL),
        P(WIDE),
        P(WIDE, None),
    )
    out_specs = (P(WIDE, None), P(), P(ALL, None))
    return jax.shard_map(local, mesh=axes, in_specs=in_specs, out_specs=out_specs, check_vma=False)
```

```python
import jax
import jax.numpy as jnp
from jax import lax
from jax.experimental import pallas as pl
from jax.experimental.pallas import tpu as pltpu
from jax.sharding import Mesh, PartitionSpec as P

F = 256
TILE = 128
TILES = 96
BLK = 4
UGRP = 16
NY, NZ, NC, NX = 4, 8, 2, 4
WIDE = ("y", "z", "c")
ALL = ("y", "z", "c", "x")
LAB = 16
BF16 = jnp.bfloat16
F32 = jnp.float32
VMEM_LIMIT = 48 * 1024 * 1024

SMEM_SPEC = pl.BlockSpec(memory_space=pltpu.SMEM)
VMEM_SPEC = pl.BlockSpec(memory_space=pltpu.VMEM)
ANY_SPEC = pl.BlockSpec(memory_space=pl.ANY)


def pack(indices, first, second):
    parts = (first, second)
    shapes = [(p["groups"], p["cap"] * TILE + LAB, TILE) for p in parts]

    def kernel(index_ref, *rest):
        groups1 = shapes[0][0]
        outs1, out2 = rest[2 : 2 + groups1], rest[2 + groups1]
        tiles1, tiles2, room1, room2, count, labels, in_sems, sems1, sem2 = rest[3 + groups1 :]
        loads = [
            pltpu.make_async_copy(rest[1], tiles2, in_sems.at[1]),
            pltpu.make_async_copy(rest[0], tiles1, in_sems.at[0]),
        ]
        for load in loads:
            load.start()
        own_y, own_c = index_ref[6 * TILES], index_ref[6 * TILES + 1]
        lane = lax.broadcasted_iota(jnp.int32, (1, TILE), 1)

        def lay(part, at, tiles_ref, room):
            groups, rows, _ = room.shape
            for g in range(groups):
                count[g] = 0
            labels[...] = jnp.full(labels.shape, float(BLK * part["dummy"]), F32)

            def step(t, carry):
                source, own, slot = (index_ref[at + i * TILES + t] for i in range(3))
                g = part["group_of"](own, own_y)
                rank = count[g]
                count[g] = rank + 1
                row = pl.multiple_of(rank * TILE, TILE)
                room[g, pl.ds(row, TILE), :] = tiles_ref[t]
                label = (BLK * part["block_of"](own, slot, own_c) + source).astype(F32)
                old = labels[pl.ds(g, 1), :]
                labels[pl.ds(g, 1), :] = jnp.where(lane == rank, label, old)
                return carry

            lax.fori_loop(0, TILES, step, 0)
            room[:, rows - LAB : rows, :] = jnp.broadcast_to(
                labels[0:groups][:, None, :], (groups, LAB, TILE)
            ).astype(BF16)

        loads[0].wait()
        lay(second, 3 * TILES, tiles2, room2)
        copies = [pltpu.make_async_copy(room2, out2, sem2)]
        copies[0].start()
        loads[1].wait()
        lay(first, 0, tiles1, room1)
        for g in range(groups1):
            copies.append(pltpu.make_async_copy(room1.at[g], outs1[g], sems1.at[g]))
            copies[-1].start()
        for copy in copies:
            copy.wait()

    out_shape = [jax.ShapeDtypeStruct(shapes[0][1:], BF16)] * shapes[0][0]
    out_shape.append(jax.ShapeDtypeStruct(shapes[1], BF16))
    most = max(shapes[0][0], shapes[1][0])
    outs = pl.pallas_call(
        kernel,
        out_shape=out_shape,
        in_specs=[SMEM_SPEC, ANY_SPEC, ANY_SPEC],
        out_specs=[ANY_SPEC] * len(out_shape),
        scratch_shapes=[
            pltpu.VMEM((TILES, TILE, TILE), BF16),
            pltpu.VMEM((TILES, TILE, TILE), BF16),
            pltpu.VMEM(shapes[0], BF16),
            pltpu.VMEM(shapes[1], BF16),
            pltpu.SMEM((most,), jnp.int32),
            pltpu.VMEM((most, TILE), F32),
            pltpu.SemaphoreType.DMA((2,)),
            pltpu.SemaphoreType.DMA((shapes[0][0],)),
            pltpu.SemaphoreType.DMA,
        ],
        compiler_params=pltpu.CompilerParams(vmem_limit_bytes=VMEM_LIMIT),
        cost_estimate=pl.CostEstimate(flops=0, bytes_accessed=16 * 1024 * 1024, transcendentals=0),
        name="pack",
    )(indices, first["tiles"], second["tiles"])
    return outs[:-1], outs[-1]


def labels_of(received, cap):
    return received[..., cap * TILE, :cap].astype(jnp.int32)


def products(labels, bases, received, blocks, order, cap, count, split_out, flip):
    many = isinstance(received, (list, tuple))
    tiles_in = list(received) if many else [received]
    groups = len(received) if many else received.shape[0]
    n_out = (split_out > 0) + (split_out < count)
    n_in, n_blocks = len(tiles_in), len(blocks)
    blocks = [b.reshape(-1, TILE, F) for b in blocks]
    starts = [sum(b.shape[0] for b in blocks[:i]) for i in range(len(blocks))]
    total = sum(b.shape[0] for b in blocks)

    def kernel(lab_ref, base_ref, order_ref, *rest):
        tile_refs, block_refs = rest[:n_in], rest[n_in : n_in + n_blocks]
        outs = rest[n_in + n_blocks : n_in + n_blocks + n_out]
        acc, room, tiles, sems, tile_sems = rest[n_in + n_blocks + n_out :]
        loads = [
            pltpu.make_async_copy(ref, room.at[pl.ds(starts[i], blocks[i].shape[0])], sems.at[i])
            for i, ref in enumerate(block_refs)
        ]
        rows = cap * TILE
        tile_loads = []
        for g in range(groups):
            source = tile_refs[g].at[pl.ds(0, rows), :] if many else tile_refs[0].at[g, pl.ds(0, rows), :]
            tile_loads.append(pltpu.make_async_copy(source, tiles.at[g], tile_sems.at[g]))
        for load in loads + tile_loads:
            load.start()
        acc[...] = jnp.zeros_like(acc)
        for load in loads:
            load.wait()

        def one(i, g, tile):
            lab = lab_ref[i]
            near = base_ref[g] + lax.rem(lab, BLK)
            far = lax.div(lab, BLK)
            if flip:
                empty = far >= total
                into = jnp.where(empty, count, near)
                block = room[order_ref[jnp.where(empty, 0, far)]]
                term = lax.dot_general(tile, block, (((0,), (0,)), ((), ())), preferred_element_type=F32)
            else:
                into = far
                term = jnp.dot(tile, room[near], preferred_element_type=F32)
            acc[into] = acc[into] + term

        for g in range(groups):

            def step(k, carry, g=g):
                row = pl.multiple_of(k * TILE, TILE)
                one(g * cap + k, g, tiles[g, pl.ds(row, TILE), :])
                return carry

            tile_loads[g].wait()
            lax.fori_loop(0, cap, step, 0, unroll=4)
        at = 0
        if split_out > 0:
            outs[at][...] = acc[0:split_out]
            at += 1
        if split_out < count:
            outs[at][...] = acc[split_out:count].astype(BF16)

    out_shape = []
    if split_out > 0:
        out_shape.append(jax.ShapeDtypeStruct((split_out, TILE, F), F32))
    if split_out < count:
        out_shape.append(jax.ShapeDtypeStruct((count - split_out, TILE, F), BF16))
    return pl.pallas_call(
        kernel,
        out_shape=out_shape,
        in_specs=[SMEM_SPEC, SMEM_SPEC, SMEM_SPEC] + [ANY_SPEC] * (n_in + n_blocks),
        out_specs=[VMEM_SPEC] * n_out,
        scratch_shapes=[
            pltpu.VMEM((count + 1, TILE, F), F32),
            pltpu.VMEM((total, TILE, F), BF16),
            pltpu.VMEM((groups, cap * TILE, TILE), BF16),
            pltpu.SemaphoreType.DMA((n_blocks,)),
            pltpu.SemaphoreType.DMA((groups,)),
        ],
        compiler_params=pltpu.CompilerParams(vmem_limit_bytes=VMEM_LIMIT),
        cost_estimate=pl.CostEstimate(
            flops=2 * groups * cap * TILE * TILE * F, bytes_accessed=12 * 1024 * 1024, transcendentals=0
        ),
        name="back_products" if flip else "products",
    )(labels, bases, order, *tiles_in, *blocks)


def all_to_all(value, axes):
    return lax.all_to_all(value, axes, split_axis=0, concat_axis=0, tiled=True)


def local(
    items,
    tile1_values,
    tile1_source,
    tile1_owner,
    tile1_slot,
    tile2_values,
    tile2_source,
    tile2_owner,
    tile2_slot,
    weight,
    bundle_degree,
    user_degree,
    cotangent,
):
    y, z, c, x = (lax.axis_index(a) for a in ALL)
    indices = jnp.concatenate(
        [
            tile1_source, tile1_owner[:, 0], tile1_slot,
            tile2_source, tile2_owner[:, 0], tile2_slot,
            jnp.stack([y, c]).astype(jnp.int32),
        ]
    )
    near1, near2 = NY, NZ * NC
    cap1, cap2 = TILE // near1, TILE // near2
    both1 = NC * NZ * BLK
    send1, send2 = pack(
        indices,
        dict(
            tiles=tile1_values,
            groups=near1, cap=cap1, dummy=both1,
            group_of=lambda own, own_y: (own // (NZ * NC) - own_y + NY) % NY,
            block_of=lambda own, slot, own_c: (((own + own_c) % NC) * NZ + (own // NC) % NZ) * BLK + slot,
        ),
        dict(
            tiles=tile2_values,
            groups=near2, cap=cap2, dummy=NY * UGRP,
            group_of=lambda own, own_y: own % (NZ * NC),
            block_of=lambda own, slot, own_c: (own // (NZ * NC)) * UGRP + slot,
        ),
    )
    rows = user_degree.shape[0] // NX
    zero = jnp.zeros((1,), jnp.int32)
    send1, send2, user_degree, cotangent = lax.optimization_barrier((send1, send2, user_degree, cotangent))
    degree = lax.dynamic_slice_in_dim(user_degree, x * rows, rows)[:, None].astype(F32)
    cot = lax.dynamic_slice_in_dim(cotangent, x * rows, rows)
    scaled_grad = (cot.astype(F32) / degree).astype(BF16)
    blocks1, got1 = [jnp.concatenate([items, scaled_grad])], [send1[0]]
    for dy in range(1, NY):
        pairs = [(a, (a + dy) % NY) for a in range(NY)]
        blocks1.append(lax.ppermute(blocks1[0], "y", pairs))
        got1.append(lax.ppermute(send1[dy], "y", pairs))
    near_grad = lax.all_gather(
        jnp.concatenate([scaled_grad] + [part[BLK * TILE :] for part in blocks1[1:]]), "x", axis=0, tiled=True
    )
    target = jnp.arange(NY * UGRP, dtype=jnp.int32)
    part = target % UGRP
    order3 = (part // BLK) * UGRP + ((y - target // UGRP + NY) % NY) * BLK + part % BLK
    labels1 = jnp.concatenate([labels_of(part, cap1) for part in got1])
    bases1 = jnp.arange(NY, dtype=jnp.int32) * (2 * BLK)
    got2 = all_to_all(send2, ("z", "c"))
    mine, other = products(labels1, bases1, got1, blocks1, zero, cap1, both1, both1 // NC, False)
    other = lax.ppermute(other, "c", [(0, 1), (1, 0)])
    part1 = (mine + other.astype(F32)).reshape(-1, F)
    got2, near_grad, part1 = lax.optimization_barrier((got2, near_grad, part1))
    summed = lax.psum_scatter(part1, "z", scatter_dimension=0, tiled=True)
    bundle_emb = (summed / bundle_degree[:, None].astype(F32)).astype(BF16)
    mixed = jnp.dot(bundle_emb, weight, preferred_element_type=F32)
    activated = jax.nn.silu(mixed).astype(BF16)
    near_act = lax.all_gather(activated, ("z", "c"), axis=0, tiled=True)

    labels2 = labels_of(got2, cap2).reshape(-1)
    senders = jnp.arange(near2, dtype=jnp.int32)
    halves = ((senders + c) % NC) * (NZ * BLK) + (senders // NC) * BLK
    mine, other = products(
        labels2, halves, got2, [near_grad], order3, cap2, NC * NZ * BLK, NZ * BLK, True
    )
    other = lax.ppermute(other, "c", [(0, 1), (1, 0)])
    both = (mine + other.astype(F32)).reshape(-1, F)
    near_act, both = lax.optimization_barrier((near_act, both))
    grad_act = lax.psum_scatter(both, "z", scatter_dimension=0, tiled=True)
    sigma = jax.nn.sigmoid(mixed)
    grad_mixed = (grad_act * sigma * (1.0 + mixed * (1.0 - sigma))).astype(BF16)
    local_grad = lax.dot_general(
        bundle_emb, grad_mixed, (((0,), (0,)), ((), ())), preferred_element_type=F32
    )
    grad_bundle = lax.dot_general(
        grad_mixed, weight, (((1,), (1,)), ((), ())), preferred_element_type=F32
    ).astype(BF16)

    part2 = products(
        labels2, senders * BLK, got2, [near_act], zero, cap2, NY * UGRP, 0, False
    )[0]
    got_part = all_to_all(part2.reshape(NY * NX, rows, F), ("y", "x"))
    gathered = jnp.sum(got_part.astype(F32), axis=0)
    user_part = (gathered / degree).astype(BF16)
    user_out = lax.all_gather(user_part, "x", axis=0, tiled=True)

    piece = jnp.sum(all_to_all(local_grad.reshape(near2, -1, F), ("z", "c")), axis=0)
    piece = jnp.sum(all_to_all(jnp.broadcast_to(piece, (NY * NX,) + piece.shape), ("y", "x")), axis=0)
    grad_weight = all_to_all(jnp.broadcast_to(piece, (near2,) + piece.shape), ("z", "c")).reshape(F, F)
    return (user_out, grad_weight, grad_bundle)


def solution(mesh):
    axes = Mesh(mesh.devices.reshape(NY, NZ, NC, NX), ALL)
    in_specs = (
        P(ALL, None),
        P(ALL, None, None),
        P(ALL),
        P(ALL, None),
        P(ALL),
        P(ALL, None, None),
        P(ALL),
        P(ALL, None),
        P(ALL),
        P(),
        P(ALL),
        P(WIDE),
        P(WIDE, None),
    )
    out_specs = (P(WIDE, None), P(), P(ALL, None))
    return jax.shard_map(local, mesh=axes, in_specs=in_specs, out_specs=out_specs, check_vma=False)
```

```python
import jax
import jax.numpy as jnp
from jax import lax
from jax.experimental import pallas as pl
from jax.experimental.pallas import tpu as pltpu
from jax.sharding import Mesh, PartitionSpec as P

F = 256
TILE = 128
TILES = 96
BLK = 4
UGRP = 16
NY, NZ, NC, NX = 4, 8, 2, 4
WIDE = ("y", "z", "c")
ALL = ("y", "z", "c", "x")
LAB = 16
BF16 = jnp.bfloat16
F32 = jnp.float32
VMEM_LIMIT = 48 * 1024 * 1024

SMEM_SPEC = pl.BlockSpec(memory_space=pltpu.SMEM)
VMEM_SPEC = pl.BlockSpec(memory_space=pltpu.VMEM)
ANY_SPEC = pl.BlockSpec(memory_space=pl.ANY)


def pack(indices, first, second):
    parts = (first, second)
    shapes = [(p["groups"], p["cap"] * TILE + LAB, TILE) for p in parts]

    def kernel(index_ref, *rest):
        groups1 = shapes[0][0]
        outs1, out2 = rest[2 : 2 + groups1], rest[2 + groups1]
        tiles1, tiles2, room1, room2, count, labels, in_sems, sems1, sem2 = rest[3 + groups1 :]
        loads = [
            pltpu.make_async_copy(rest[1], tiles2, in_sems.at[1]),
            pltpu.make_async_copy(rest[0], tiles1, in_sems.at[0]),
        ]
        for load in loads:
            load.start()
        own_y, own_c = index_ref[6 * TILES], index_ref[6 * TILES + 1]
        lane = lax.broadcasted_iota(jnp.int32, (1, TILE), 1)

        def lay(part, at, tiles_ref, room):
            groups, rows, _ = room.shape
            for g in range(groups):
                count[g] = 0
            labels[...] = jnp.full(labels.shape, float(BLK * part["dummy"]), F32)

            def step(t, carry):
                source, own, slot = (index_ref[at + i * TILES + t] for i in range(3))
                g = part["group_of"](own, own_y)
                rank = count[g]
                count[g] = rank + 1
                row = pl.multiple_of(rank * TILE, TILE)
                room[g, pl.ds(row, TILE), :] = tiles_ref[t]
                label = (BLK * part["block_of"](own, slot, own_c) + source).astype(F32)
                old = labels[pl.ds(g, 1), :]
                labels[pl.ds(g, 1), :] = jnp.where(lane == rank, label, old)
                return carry

            lax.fori_loop(0, TILES, step, 0)
            room[:, rows - LAB : rows, :] = jnp.broadcast_to(
                labels[0:groups][:, None, :], (groups, LAB, TILE)
            ).astype(BF16)

        loads[0].wait()
        lay(second, 3 * TILES, tiles2, room2)
        copies = [pltpu.make_async_copy(room2, out2, sem2)]
        copies[0].start()
        loads[1].wait()
        lay(first, 0, tiles1, room1)
        for g in range(groups1):
            copies.append(pltpu.make_async_copy(room1.at[g], outs1[g], sems1.at[g]))
            copies[-1].start()
        for copy in copies:
            copy.wait()

    out_shape = [jax.ShapeDtypeStruct(shapes[0][1:], BF16)] * shapes[0][0]
    out_shape.append(jax.ShapeDtypeStruct(shapes[1], BF16))
    most = max(shapes[0][0], shapes[1][0])
    outs = pl.pallas_call(
        kernel,
        out_shape=out_shape,
        in_specs=[SMEM_SPEC, ANY_SPEC, ANY_SPEC],
        out_specs=[ANY_SPEC] * len(out_shape),
        scratch_shapes=[
            pltpu.VMEM((TILES, TILE, TILE), BF16),
            pltpu.VMEM((TILES, TILE, TILE), BF16),
            pltpu.VMEM(shapes[0], BF16),
            pltpu.VMEM(shapes[1], BF16),
            pltpu.SMEM((most,), jnp.int32),
            pltpu.VMEM((most, TILE), F32),
            pltpu.SemaphoreType.DMA((2,)),
            pltpu.SemaphoreType.DMA((shapes[0][0],)),
            pltpu.SemaphoreType.DMA,
        ],
        compiler_params=pltpu.CompilerParams(vmem_limit_bytes=60 * 1024 * 1024),
        cost_estimate=pl.CostEstimate(flops=0, bytes_accessed=16 * 1024 * 1024, transcendentals=0),
        name="pack",
    )(indices, first["tiles"], second["tiles"])
    return outs[:-1], outs[-1]


def labels_of(received, cap):
    return received[..., cap * TILE, :cap].astype(jnp.int32)


def products(labels, bases, received, blocks, order, cap, count, split_out, flip):
    many = isinstance(received, (list, tuple))
    tiles_in = list(received) if many else [received]
    groups = len(received) if many else received.shape[0]
    n_out = (split_out > 0) + (split_out < count)
    n_in, n_blocks = len(tiles_in), len(blocks)
    blocks = [b.reshape(-1, TILE, F) for b in blocks]
    starts = [sum(b.shape[0] for b in blocks[:i]) for i in range(len(blocks))]
    total = sum(b.shape[0] for b in blocks)

    def kernel(lab_ref, base_ref, order_ref, *rest):
        tile_refs, block_refs = rest[:n_in], rest[n_in : n_in + n_blocks]
        outs = rest[n_in + n_blocks : n_in + n_blocks + n_out]
        acc, room, tiles, sems, tile_sems = rest[n_in + n_blocks + n_out :]
        loads = [
            pltpu.make_async_copy(ref, room.at[pl.ds(starts[i], blocks[i].shape[0])], sems.at[i])
            for i, ref in enumerate(block_refs)
        ]
        rows = cap * TILE
        tile_loads = []
        for g in range(groups):
            source = tile_refs[g].at[pl.ds(0, rows), :] if many else tile_refs[0].at[g, pl.ds(0, rows), :]
            tile_loads.append(pltpu.make_async_copy(source, tiles.at[g], tile_sems.at[g]))
        for load in loads + tile_loads:
            load.start()
        acc[...] = jnp.zeros_like(acc)
        for load in loads:
            load.wait()

        def one(i, g, tile):
            lab = lab_ref[i]
            near = base_ref[g] + lax.rem(lab, BLK)
            far = lax.div(lab, BLK)
            if flip:
                empty = far >= total
                into = jnp.where(empty, count, near)
                block = room[order_ref[jnp.where(empty, 0, far)]]
                term = lax.dot_general(tile, block, (((0,), (0,)), ((), ())), preferred_element_type=F32)
            else:
                into = far
                term = jnp.dot(tile, room[near], preferred_element_type=F32)
            acc[into] = acc[into] + term

        for g in range(groups):

            def step(k, carry, g=g):
                row = pl.multiple_of(k * TILE, TILE)
                one(g * cap + k, g, tiles[g, pl.ds(row, TILE), :])
                return carry

            tile_loads[g].wait()
            lax.fori_loop(0, cap, step, 0, unroll=4)
        at = 0
        if split_out > 0:
            outs[at][...] = acc[0:split_out]
            at += 1
        if split_out < count:
            outs[at][...] = acc[split_out:count].astype(BF16)

    out_shape = []
    if split_out > 0:
        out_shape.append(jax.ShapeDtypeStruct((split_out, TILE, F), F32))
    if split_out < count:
        out_shape.append(jax.ShapeDtypeStruct((count - split_out, TILE, F), BF16))
    return pl.pallas_call(
        kernel,
        out_shape=out_shape,
        in_specs=[SMEM_SPEC, SMEM_SPEC, SMEM_SPEC] + [ANY_SPEC] * (n_in + n_blocks),
        out_specs=[VMEM_SPEC] * n_out,
        scratch_shapes=[
            pltpu.VMEM((count + 1, TILE, F), F32),
            pltpu.VMEM((total, TILE, F), BF16),
            pltpu.VMEM((groups, cap * TILE, TILE), BF16),
            pltpu.SemaphoreType.DMA((n_blocks,)),
            pltpu.SemaphoreType.DMA((groups,)),
        ],
        compiler_params=pltpu.CompilerParams(vmem_limit_bytes=VMEM_LIMIT),
        cost_estimate=pl.CostEstimate(
            flops=2 * groups * cap * TILE * TILE * F, bytes_accessed=12 * 1024 * 1024, transcendentals=0
        ),
        name="back_products" if flip else "products",
    )(labels, bases, order, *tiles_in, *blocks)


def all_to_all(value, axes):
    return lax.all_to_all(value, axes, split_axis=0, concat_axis=0, tiled=True)


def local(
    items,
    tile1_values,
    tile1_source,
    tile1_owner,
    tile1_slot,
    tile2_values,
    tile2_source,
    tile2_owner,
    tile2_slot,
    weight,
    bundle_degree,
    user_degree,
    cotangent,
):
    y, z, c, x = (lax.axis_index(a) for a in ALL)
    indices = jnp.concatenate(
        [
            tile1_source, tile1_owner[:, 0], tile1_slot,
            tile2_source, tile2_owner[:, 0], tile2_slot,
            jnp.stack([y, c]).astype(jnp.int32),
        ]
    )
    near1, near2 = NY, NZ * NC
    cap1, cap2 = TILE // near1, TILE // near2
    both1 = NC * NZ * BLK
    send1, send2 = pack(
        indices,
        dict(
            tiles=tile1_values,
            groups=near1, cap=cap1, dummy=both1,
            group_of=lambda own, own_y: (own // (NZ * NC) - own_y + NY) % NY,
            block_of=lambda own, slot, own_c: (((own + own_c) % NC) * NZ + (own // NC) % NZ) * BLK + slot,
        ),
        dict(
            tiles=tile2_values,
            groups=near2, cap=cap2, dummy=NY * UGRP,
            group_of=lambda own, own_y: own % (NZ * NC),
            block_of=lambda own, slot, own_c: (own // (NZ * NC)) * UGRP + slot,
        ),
    )
    rows = user_degree.shape[0] // NX
    zero = jnp.zeros((1,), jnp.int32)
    send1, send2, user_degree, cotangent = lax.optimization_barrier((send1, send2, user_degree, cotangent))
    degree = lax.dynamic_slice_in_dim(user_degree, x * rows, rows)[:, None].astype(F32)
    cot = lax.dynamic_slice_in_dim(cotangent, x * rows, rows)
    scaled_grad = (cot.astype(F32) / degree).astype(BF16)
    near = lax.all_gather(jnp.concatenate([items, scaled_grad]), "y", axis=0, tiled=True)
    column = near.reshape(NY, -1, F)[:, BLK * TILE :]
    near_grad = lax.all_gather(column.reshape(-1, F), "x", axis=0, tiled=True)
    got1 = [send1[0]]
    for dy in range(1, NY):
        got1.append(lax.ppermute(send1[dy], "y", [(a, (a + dy) % NY) for a in range(NY)]))
    target = jnp.arange(NY * UGRP, dtype=jnp.int32)
    part = target % UGRP
    order3 = (part // BLK) * UGRP + (target // UGRP) * BLK + part % BLK
    labels1 = jnp.concatenate([labels_of(part, cap1) for part in got1])
    bases1 = ((y - jnp.arange(NY, dtype=jnp.int32) + NY) % NY) * (2 * BLK)
    got2 = all_to_all(send2, ("z", "c"))
    mine, other = products(labels1, bases1, got1, [near], zero, cap1, both1, both1 // NC, False)
    other = lax.ppermute(other, "c", [(0, 1), (1, 0)])
    part1 = (mine + other.astype(F32)).reshape(-1, F)
    got2, near_grad, part1 = lax.optimization_barrier((got2, near_grad, part1))
    summed = lax.psum_scatter(part1, "z", scatter_dimension=0, tiled=True)
    bundle_emb = (summed / bundle_degree[:, None].astype(F32)).astype(BF16)
    mixed = jnp.dot(bundle_emb, weight, preferred_element_type=F32)
    activated = jax.nn.silu(mixed).astype(BF16)
    near_act = lax.all_gather(activated, ("z", "c"), axis=0, tiled=True)

    labels2 = labels_of(got2, cap2).reshape(-1)
    senders = jnp.arange(near2, dtype=jnp.int32)
    halves = ((senders + c) % NC) * (NZ * BLK) + (senders // NC) * BLK
    mine, other = products(
        labels2, halves, got2, [near_grad], order3, cap2, NC * NZ * BLK, NZ * BLK, True
    )
    other = lax.ppermute(other, "c", [(0, 1), (1, 0)])
    both = (mine + other.astype(F32)).reshape(-1, F)
    near_act, both = lax.optimization_barrier((near_act, both))
    grad_act = lax.psum_scatter(both, "z", scatter_dimension=0, tiled=True)
    sigma = jax.nn.sigmoid(mixed)
    grad_mixed = (grad_act * sigma * (1.0 + mixed * (1.0 - sigma))).astype(BF16)
    local_grad = lax.dot_general(
        bundle_emb, grad_mixed, (((0,), (0,)), ((), ())), preferred_element_type=F32
    )
    grad_bundle = lax.dot_general(
        grad_mixed, weight, (((1,), (1,)), ((), ())), preferred_element_type=F32
    ).astype(BF16)

    part2 = products(
        labels2, senders * BLK, got2, [near_act], zero, cap2, NY * UGRP, 0, False
    )[0]
    got_part = all_to_all(part2.reshape(NY * NX, rows, F), ("y", "x"))
    gathered = jnp.sum(got_part.astype(F32), axis=0)
    user_part = (gathered / degree).astype(BF16)
    user_out = lax.all_gather(user_part, "x", axis=0, tiled=True)

    piece = jnp.sum(all_to_all(local_grad.reshape(near2, -1, F), ("z", "c")), axis=0)
    piece = jnp.sum(all_to_all(jnp.broadcast_to(piece, (NY * NX,) + piece.shape), ("y", "x")), axis=0)
    grad_weight = all_to_all(jnp.broadcast_to(piece, (near2,) + piece.shape), ("z", "c")).reshape(F, F)
    return (user_out, grad_weight, grad_bundle)


def solution(mesh):
    axes = Mesh(mesh.devices.reshape(NY, NZ, NC, NX), ALL)
    in_specs = (
        P(ALL, None),
        P(ALL, None, None),
        P(ALL),
        P(ALL, None),
        P(ALL),
        P(ALL, None, None),
        P(ALL),
        P(ALL, None),
        P(ALL),
        P(),
        P(ALL),
        P(WIDE),
        P(WIDE, None),
    )
    out_specs = (P(WIDE, None), P(), P(ALL, None))
    return jax.shard_map(local, mesh=axes, in_specs=in_specs, out_specs=out_specs, check_vma=False)
```

```python
import jax
import jax.numpy as jnp
from jax import lax
from jax.experimental import pallas as pl
from jax.experimental.pallas import tpu as pltpu
from jax.sharding import Mesh, PartitionSpec as P

F = 256
TILE = 128
TILES = 96
BLK = 4
UGRP = 16
NY, NZ, NC, NX = 4, 8, 2, 4
WIDE = ("y", "z", "c")
ALL = ("y", "z", "c", "x")
LAB = 16
BF16 = jnp.bfloat16
F32 = jnp.float32
VMEM_LIMIT = 48 * 1024 * 1024

SMEM_SPEC = pl.BlockSpec(memory_space=pltpu.SMEM)
VMEM_SPEC = pl.BlockSpec(memory_space=pltpu.VMEM)
ANY_SPEC = pl.BlockSpec(memory_space=pl.ANY)


def pack(indices, first, second):
    parts = (first, second)
    shapes = [(p["groups"], p["cap"] * TILE + LAB, TILE) for p in parts]

    def kernel(index_ref, *rest):
        groups1 = shapes[0][0]
        outs1, out2 = rest[2 : 2 + groups1], rest[2 + groups1]
        tiles1, tiles2, room1, room2, count, labels, in_sems, sems1, sem2 = rest[3 + groups1 :]
        loads = [
            pltpu.make_async_copy(rest[1], tiles2, in_sems.at[1]),
            pltpu.make_async_copy(rest[0], tiles1, in_sems.at[0]),
        ]
        for load in loads:
            load.start()
        own_y, own_c = index_ref[6 * TILES], index_ref[6 * TILES + 1]
        lane = lax.broadcasted_iota(jnp.int32, (1, TILE), 1)

        def lay(part, at, tiles_ref, room):
            groups, rows, _ = room.shape
            for g in range(groups):
                count[g] = 0
            labels[...] = jnp.full(labels.shape, float(BLK * part["dummy"]), F32)

            def step(t, carry):
                source, own, slot = (index_ref[at + i * TILES + t] for i in range(3))
                g = part["group_of"](own, own_y)
                rank = count[g]
                count[g] = rank + 1
                row = pl.multiple_of(rank * TILE, TILE)
                room[g, pl.ds(row, TILE), :] = tiles_ref[t]
                label = (BLK * part["block_of"](own, slot, own_c) + source).astype(F32)
                old = labels[pl.ds(g, 1), :]
                labels[pl.ds(g, 1), :] = jnp.where(lane == rank, label, old)
                return carry

            lax.fori_loop(0, TILES, step, 0)
            room[:, rows - LAB : rows, :] = jnp.broadcast_to(
                labels[0:groups][:, None, :], (groups, LAB, TILE)
            ).astype(BF16)

        loads[0].wait()
        lay(second, 3 * TILES, tiles2, room2)
        copies = [pltpu.make_async_copy(room2, out2, sem2)]
        copies[0].start()
        loads[1].wait()
        lay(first, 0, tiles1, room1)
        for g in range(groups1):
            copies.append(pltpu.make_async_copy(room1.at[g], outs1[g], sems1.at[g]))
            copies[-1].start()
        for copy in copies:
            copy.wait()

    out_shape = [jax.ShapeDtypeStruct(shapes[0][1:], BF16)] * shapes[0][0]
    out_shape.append(jax.ShapeDtypeStruct(shapes[1], BF16))
    most = max(shapes[0][0], shapes[1][0])
    outs = pl.pallas_call(
        kernel,
        out_shape=out_shape,
        in_specs=[SMEM_SPEC, ANY_SPEC, ANY_SPEC],
        out_specs=[ANY_SPEC] * len(out_shape),
        scratch_shapes=[
            pltpu.VMEM((TILES, TILE, TILE), BF16),
            pltpu.VMEM((TILES, TILE, TILE), BF16),
            pltpu.VMEM(shapes[0], BF16),
            pltpu.VMEM(shapes[1], BF16),
            pltpu.SMEM((most,), jnp.int32),
            pltpu.VMEM((most, TILE), F32),
            pltpu.SemaphoreType.DMA((2,)),
            pltpu.SemaphoreType.DMA((shapes[0][0],)),
            pltpu.SemaphoreType.DMA,
        ],
        compiler_params=pltpu.CompilerParams(vmem_limit_bytes=60 * 1024 * 1024),
        cost_estimate=pl.CostEstimate(flops=0, bytes_accessed=16 * 1024 * 1024, transcendentals=0),
        name="pack",
    )(indices, first["tiles"], second["tiles"])
    return outs[:-1], outs[-1]


def labels_of(received, cap):
    return received[..., cap * TILE, :cap].astype(jnp.int32)


def products(labels, bases, received, blocks, order, cap, count, split_out, flip):
    many = isinstance(received, (list, tuple))
    tiles_in = list(received) if many else [received]
    groups = len(received) if many else received.shape[0]
    n_out = (split_out > 0) + (split_out < count)
    n_in, n_blocks = len(tiles_in), len(blocks)
    blocks = [b.reshape(-1, TILE, F) for b in blocks]
    starts = [sum(b.shape[0] for b in blocks[:i]) for i in range(len(blocks))]
    total = sum(b.shape[0] for b in blocks)

    def kernel(lab_ref, base_ref, order_ref, *rest):
        tile_refs, block_refs = rest[:n_in], rest[n_in : n_in + n_blocks]
        outs = rest[n_in + n_blocks : n_in + n_blocks + n_out]
        acc, room, tiles, sems, tile_sems = rest[n_in + n_blocks + n_out :]
        loads = [
            pltpu.make_async_copy(ref, room.at[pl.ds(starts[i], blocks[i].shape[0])], sems.at[i])
            for i, ref in enumerate(block_refs)
        ]
        rows = cap * TILE
        tile_loads = []
        for g in range(groups):
            source = tile_refs[g].at[pl.ds(0, rows), :] if many else tile_refs[0].at[g, pl.ds(0, rows), :]
            tile_loads.append(pltpu.make_async_copy(source, tiles.at[g], tile_sems.at[g]))
        for load in loads + tile_loads:
            load.start()
        acc[...] = jnp.zeros_like(acc)
        for load in loads:
            load.wait()

        def one(i, g, tile):
            lab = lab_ref[i]
            near = base_ref[g] + lax.rem(lab, BLK)
            far = lax.div(lab, BLK)
            if flip:
                empty = far >= total
                into = jnp.where(empty, count, near)
                block = room[order_ref[jnp.where(empty, 0, far)]]
                term = lax.dot_general(tile, block, (((0,), (0,)), ((), ())), preferred_element_type=F32)
            else:
                into = far
                term = jnp.dot(tile, room[near], preferred_element_type=F32)
            acc[into] = acc[into] + term

        for g in range(groups):

            def step(k, carry, g=g):
                row = pl.multiple_of(k * TILE, TILE)
                one(g * cap + k, g, tiles[g, pl.ds(row, TILE), :])
                return carry

            tile_loads[g].wait()
            lax.fori_loop(0, cap, step, 0, unroll=4)
        at = 0
        if split_out > 0:
            outs[at][...] = acc[0:split_out]
            at += 1
        if split_out < count:
            outs[at][...] = acc[split_out:count].astype(BF16)

    out_shape = []
    if split_out > 0:
        out_shape.append(jax.ShapeDtypeStruct((split_out, TILE, F), F32))
    if split_out < count:
        out_shape.append(jax.ShapeDtypeStruct((count - split_out, TILE, F), BF16))
    return pl.pallas_call(
        kernel,
        out_shape=out_shape,
        in_specs=[SMEM_SPEC, SMEM_SPEC, SMEM_SPEC] + [ANY_SPEC] * (n_in + n_blocks),
        out_specs=[VMEM_SPEC] * n_out,
        scratch_shapes=[
            pltpu.VMEM((count + 1, TILE, F), F32),
            pltpu.VMEM((total, TILE, F), BF16),
            pltpu.VMEM((groups, cap * TILE, TILE), BF16),
            pltpu.SemaphoreType.DMA((n_blocks,)),
            pltpu.SemaphoreType.DMA((groups,)),
        ],
        compiler_params=pltpu.CompilerParams(vmem_limit_bytes=VMEM_LIMIT),
        cost_estimate=pl.CostEstimate(
            flops=2 * groups * cap * TILE * TILE * F, bytes_accessed=12 * 1024 * 1024, transcendentals=0
        ),
        name="back_products" if flip else "products",
    )(labels, bases, order, *tiles_in, *blocks)


def all_to_all(value, axes):
    return lax.all_to_all(value, axes, split_axis=0, concat_axis=0, tiled=True)


def local(
    items,
    tile1_values,
    tile1_source,
    tile1_owner,
    tile1_slot,
    tile2_values,
    tile2_source,
    tile2_owner,
    tile2_slot,
    weight,
    bundle_degree,
    user_degree,
    cotangent,
):
    y, z, c, x = (lax.axis_index(a) for a in ALL)
    indices = jnp.concatenate(
        [
            tile1_source, tile1_owner[:, 0], tile1_slot,
            tile2_source, tile2_owner[:, 0], tile2_slot,
            jnp.stack([y, c]).astype(jnp.int32),
        ]
    )
    near1, near2 = NY, NZ * NC
    cap1, cap2 = TILE // near1, TILE // near2
    both1 = NC * NZ * BLK
    send1, send2 = pack(
        indices,
        dict(
            tiles=tile1_values,
            groups=near1, cap=cap1, dummy=both1,
            group_of=lambda own, own_y: (own // (NZ * NC) - own_y + NY) % NY,
            block_of=lambda own, slot, own_c: (((own + own_c) % NC) * NZ + (own // NC) % NZ) * BLK + slot,
        ),
        dict(
            tiles=tile2_values,
            groups=near2, cap=cap2, dummy=NY * UGRP,
            group_of=lambda own, own_y: own % (NZ * NC),
            block_of=lambda own, slot, own_c: (own // (NZ * NC)) * UGRP + slot,
        ),
    )
    rows = user_degree.shape[0] // NX
    zero = jnp.zeros((1,), jnp.int32)
    send1, send2, user_degree, cotangent = lax.optimization_barrier((send1, send2, user_degree, cotangent))
    degree = lax.dynamic_slice_in_dim(user_degree, x * rows, rows)[:, None].astype(F32)
    cot = lax.dynamic_slice_in_dim(cotangent, x * rows, rows)
    scaled_grad = (cot.astype(F32) / degree).astype(BF16)
    near = lax.all_gather(jnp.concatenate([items, scaled_grad]), "y", axis=0, tiled=True)
    got1 = [send1[0]]
    for dy in range(1, NY):
        got1.append(lax.ppermute(send1[dy], "y", [(a, (a + dy) % NY) for a in range(NY)]))
    near, got1[2], got1[3] = lax.optimization_barrier((near, got1[2], got1[3]))
    column = near.reshape(NY, -1, F)[:, BLK * TILE :]
    near_grad = lax.all_gather(column.reshape(-1, F), "x", axis=0, tiled=True)
    target = jnp.arange(NY * UGRP, dtype=jnp.int32)
    part = target % UGRP
    order3 = (part // BLK) * UGRP + (target // UGRP) * BLK + part % BLK
    labels1 = jnp.concatenate([labels_of(part, cap1) for part in got1])
    bases1 = ((y - jnp.arange(NY, dtype=jnp.int32) + NY) % NY) * (2 * BLK)
    got2 = all_to_all(send2, ("z", "c"))
    mine, other = products(labels1, bases1, got1, [near], zero, cap1, both1, both1 // NC, False)
    other = lax.ppermute(other, "c", [(0, 1), (1, 0)])
    part1 = (mine + other.astype(F32)).reshape(-1, F)
    got2, near_grad, part1 = lax.optimization_barrier((got2, near_grad, part1))
    summed = lax.psum_scatter(part1, "z", scatter_dimension=0, tiled=True)
    bundle_emb = (summed / bundle_degree[:, None].astype(F32)).astype(BF16)
    mixed = jnp.dot(bundle_emb, weight, preferred_element_type=F32)
    activated = jax.nn.silu(mixed).astype(BF16)
    near_act = lax.all_gather(activated, ("z", "c"), axis=0, tiled=True)

    labels2 = labels_of(got2, cap2).reshape(-1)
    senders = jnp.arange(near2, dtype=jnp.int32)
    halves = ((senders + c) % NC) * (NZ * BLK) + (senders // NC) * BLK
    mine, other = products(
        labels2, halves, got2, [near_grad], order3, cap2, NC * NZ * BLK, NZ * BLK, True
    )
    other = lax.ppermute(other, "c", [(0, 1), (1, 0)])
    both = (mine + other.astype(F32)).reshape(-1, F)
    near_act, both = lax.optimization_barrier((near_act, both))
    grad_act = lax.psum_scatter(both, "z", scatter_dimension=0, tiled=True)
    sigma = jax.nn.sigmoid(mixed)
    grad_mixed = (grad_act * sigma * (1.0 + mixed * (1.0 - sigma))).astype(BF16)
    local_grad = lax.dot_general(
        bundle_emb, grad_mixed, (((0,), (0,)), ((), ())), preferred_element_type=F32
    )
    grad_bundle = lax.dot_general(
        grad_mixed, weight, (((1,), (1,)), ((), ())), preferred_element_type=F32
    ).astype(BF16)

    part2 = products(
        labels2, senders * BLK, got2, [near_act], zero, cap2, NY * UGRP, 0, False
    )[0]
    got_part = all_to_all(part2.reshape(NY * NX, rows, F), ("y", "x"))
    gathered = jnp.sum(got_part.astype(F32), axis=0)
    user_part = (gathered / degree).astype(BF16)
    user_out = lax.all_gather(user_part, "x", axis=0, tiled=True)

    piece = jnp.sum(all_to_all(local_grad.reshape(near2, -1, F), ("z", "c")), axis=0)
    piece = jnp.sum(all_to_all(jnp.broadcast_to(piece, (NY * NX,) + piece.shape), ("y", "x")), axis=0)
    grad_weight = all_to_all(jnp.broadcast_to(piece, (near2,) + piece.shape), ("z", "c")).reshape(F, F)
    return (user_out, grad_weight, grad_bundle)


def solution(mesh):
    axes = Mesh(mesh.devices.reshape(NY, NZ, NC, NX), ALL)
    in_specs = (
        P(ALL, None),
        P(ALL, None, None),
        P(ALL),
        P(ALL, None),
        P(ALL),
        P(ALL, None, None),
        P(ALL),
        P(ALL, None),
        P(ALL),
        P(),
        P(ALL),
        P(WIDE),
        P(WIDE, None),
    )
    out_specs = (P(WIDE, None), P(), P(ALL, None))
    return jax.shard_map(local, mesh=axes, in_specs=in_specs, out_specs=out_specs, check_vma=False)
```

```python
import jax
import jax.numpy as jnp
from jax import lax
from jax.experimental import pallas as pl
from jax.experimental.pallas import tpu as pltpu
from jax.sharding import Mesh, PartitionSpec as P

F = 256
TILE = 128
TILES = 96
BLK = 4
UGRP = 16
NY, NZ, NC, NX = 4, 8, 2, 4
WIDE = ("y", "z", "c")
ALL = ("y", "z", "c", "x")
LAB = 16
BF16 = jnp.bfloat16
F32 = jnp.float32
VMEM_LIMIT = 48 * 1024 * 1024

SMEM_SPEC = pl.BlockSpec(memory_space=pltpu.SMEM)
VMEM_SPEC = pl.BlockSpec(memory_space=pltpu.VMEM)
ANY_SPEC = pl.BlockSpec(memory_space=pl.ANY)


def pack(indices, first, second):
    parts = (first, second)
    shapes = [(p["groups"], p["cap"] * TILE + LAB, TILE) for p in parts]

    def kernel(index_ref, *rest):
        groups1 = shapes[0][0]
        outs1, out2 = rest[2 : 2 + groups1], rest[2 + groups1]
        tiles1, tiles2, room1, room2, count, labels, in_sems, sems1, sem2 = rest[3 + groups1 :]
        loads = [
            pltpu.make_async_copy(rest[1], tiles2, in_sems.at[1]),
            pltpu.make_async_copy(rest[0], tiles1, in_sems.at[0]),
        ]
        for load in loads:
            load.start()
        own_y, own_c = index_ref[6 * TILES], index_ref[6 * TILES + 1]
        lane = lax.broadcasted_iota(jnp.int32, (1, TILE), 1)

        def lay(part, at, tiles_ref, room):
            groups, rows, _ = room.shape
            for g in range(groups):
                count[g] = 0
            labels[...] = jnp.full(labels.shape, float(BLK * part["dummy"]), F32)

            def step(t, carry):
                source, own, slot = (index_ref[at + i * TILES + t] for i in range(3))
                g = part["group_of"](own, own_y)
                rank = count[g]
                count[g] = rank + 1
                row = pl.multiple_of(rank * TILE, TILE)
                room[g, pl.ds(row, TILE), :] = tiles_ref[t]
                label = (BLK * part["block_of"](own, slot, own_c) + source).astype(F32)
                old = labels[pl.ds(g, 1), :]
                labels[pl.ds(g, 1), :] = jnp.where(lane == rank, label, old)
                return carry

            lax.fori_loop(0, TILES, step, 0)
            room[:, rows - LAB : rows, :] = jnp.broadcast_to(
                labels[0:groups][:, None, :], (groups, LAB, TILE)
            ).astype(BF16)

        loads[0].wait()
        lay(second, 3 * TILES, tiles2, room2)
        copies = [pltpu.make_async_copy(room2, out2, sem2)]
        copies[0].start()
        loads[1].wait()
        lay(first, 0, tiles1, room1)
        for g in range(groups1):
            copies.append(pltpu.make_async_copy(room1.at[g], outs1[g], sems1.at[g]))
            copies[-1].start()
        for copy in copies:
            copy.wait()

    out_shape = [jax.ShapeDtypeStruct(shapes[0][1:], BF16)] * shapes[0][0]
    out_shape.append(jax.ShapeDtypeStruct(shapes[1], BF16))
    most = max(shapes[0][0], shapes[1][0])
    outs = pl.pallas_call(
        kernel,
        out_shape=out_shape,
        in_specs=[SMEM_SPEC, ANY_SPEC, ANY_SPEC],
        out_specs=[ANY_SPEC] * len(out_shape),
        scratch_shapes=[
            pltpu.VMEM((TILES, TILE, TILE), BF16),
            pltpu.VMEM((TILES, TILE, TILE), BF16),
            pltpu.VMEM(shapes[0], BF16),
            pltpu.VMEM(shapes[1], BF16),
            pltpu.SMEM((most,), jnp.int32),
            pltpu.VMEM((most, TILE), F32),
            pltpu.SemaphoreType.DMA((2,)),
            pltpu.SemaphoreType.DMA((shapes[0][0],)),
            pltpu.SemaphoreType.DMA,
        ],
        compiler_params=pltpu.CompilerParams(vmem_limit_bytes=VMEM_LIMIT),
        cost_estimate=pl.CostEstimate(flops=0, bytes_accessed=16 * 1024 * 1024, transcendentals=0),
        name="pack",
    )(indices, first["tiles"], second["tiles"])
    return outs[:-1], outs[-1]


def labels_of(received, cap):
    return received[..., cap * TILE, :cap].astype(jnp.int32)


def products(labels, bases, received, blocks, order, cap, count, split_out, flip):
    many = isinstance(received, (list, tuple))
    tiles_in = list(received) if many else [received]
    groups = len(received) if many else received.shape[0]
    n_out = (split_out > 0) + (split_out < count)
    n_in, n_blocks = len(tiles_in), len(blocks)
    blocks = [b.reshape(-1, TILE, F) for b in blocks]
    starts = [sum(b.shape[0] for b in blocks[:i]) for i in range(len(blocks))]
    total = sum(b.shape[0] for b in blocks)

    def kernel(lab_ref, base_ref, order_ref, *rest):
        tile_refs, block_refs = rest[:n_in], rest[n_in : n_in + n_blocks]
        outs = rest[n_in + n_blocks : n_in + n_blocks + n_out]
        acc, room, tiles, sems, tile_sems = rest[n_in + n_blocks + n_out :]
        loads = [
            pltpu.make_async_copy(ref, room.at[pl.ds(starts[i], blocks[i].shape[0])], sems.at[i])
            for i, ref in enumerate(block_refs)
        ]
        rows = cap * TILE
        tile_loads = []
        for g in range(groups):
            source = tile_refs[g].at[pl.ds(0, rows), :] if many else tile_refs[0].at[g, pl.ds(0, rows), :]
            tile_loads.append(pltpu.make_async_copy(source, tiles.at[g], tile_sems.at[g]))
        for load in loads + tile_loads:
            load.start()
        acc[...] = jnp.zeros_like(acc)
        for load in loads:
            load.wait()

        def one(i, g, tile):
            lab = lab_ref[i]
            near = base_ref[g] + lax.rem(lab, BLK)
            far = lax.div(lab, BLK)
            if flip:
                empty = far >= total
                into = jnp.where(empty, count, near)
                block = room[order_ref[jnp.where(empty, 0, far)]]
                term = lax.dot_general(tile, block, (((0,), (0,)), ((), ())), preferred_element_type=F32)
            else:
                into = far
                term = jnp.dot(tile, room[near], preferred_element_type=F32)
            acc[into] = acc[into] + term

        for g in range(groups):

            def step(k, carry, g=g):
                row = pl.multiple_of(k * TILE, TILE)
                one(g * cap + k, g, tiles[g, pl.ds(row, TILE), :])
                return carry

            tile_loads[g].wait()
            lax.fori_loop(0, cap, step, 0, unroll=4)
        at = 0
        if split_out > 0:
            outs[at][...] = acc[0:split_out]
            at += 1
        if split_out < count:
            outs[at][...] = acc[split_out:count].astype(BF16)

    out_shape = []
    if split_out > 0:
        out_shape.append(jax.ShapeDtypeStruct((split_out, TILE, F), F32))
    if split_out < count:
        out_shape.append(jax.ShapeDtypeStruct((count - split_out, TILE, F), BF16))
    return pl.pallas_call(
        kernel,
        out_shape=out_shape,
        in_specs=[SMEM_SPEC, SMEM_SPEC, SMEM_SPEC] + [ANY_SPEC] * (n_in + n_blocks),
        out_specs=[VMEM_SPEC] * n_out,
        scratch_shapes=[
            pltpu.VMEM((count + 1, TILE, F), F32),
            pltpu.VMEM((total, TILE, F), BF16),
            pltpu.VMEM((groups, cap * TILE, TILE), BF16),
            pltpu.SemaphoreType.DMA((n_blocks,)),
            pltpu.SemaphoreType.DMA((groups,)),
        ],
        compiler_params=pltpu.CompilerParams(vmem_limit_bytes=VMEM_LIMIT),
        cost_estimate=pl.CostEstimate(
            flops=2 * groups * cap * TILE * TILE * F, bytes_accessed=12 * 1024 * 1024, transcendentals=0
        ),
        name="back_products" if flip else "products",
    )(labels, bases, order, *tiles_in, *blocks)


def all_to_all(value, axes):
    return lax.all_to_all(value, axes, split_axis=0, concat_axis=0, tiled=True)


def local(
    items,
    tile1_values,
    tile1_source,
    tile1_owner,
    tile1_slot,
    tile2_values,
    tile2_source,
    tile2_owner,
    tile2_slot,
    weight,
    bundle_degree,
    user_degree,
    cotangent,
):
    y, z, c, x = (lax.axis_index(a) for a in ALL)
    indices = jnp.concatenate(
        [
            tile1_source, tile1_owner[:, 0], tile1_slot,
            tile2_source, tile2_owner[:, 0], tile2_slot,
            jnp.stack([y, c]).astype(jnp.int32),
        ]
    )
    near1, near2 = NY, NZ * NC
    cap1, cap2 = TILE // near1, TILE // near2
    both1 = NC * NZ * BLK
    send1, send2 = pack(
        indices,
        dict(
            tiles=tile1_values,
            groups=near1, cap=cap1, dummy=both1,
            group_of=lambda own, own_y: (own // (NZ * NC) - own_y + NY) % NY,
            block_of=lambda own, slot, own_c: (((own + own_c) % NC) * NZ + (own // NC) % NZ) * BLK + slot,
        ),
        dict(
            tiles=tile2_values,
            groups=near2, cap=cap2, dummy=NY * UGRP,
            group_of=lambda own, own_y: own % (NZ * NC),
            block_of=lambda own, slot, own_c: (own // (NZ * NC)) * UGRP + slot,
        ),
    )
    zero = jnp.zeros((1,), jnp.int32)
    along_y = [[(a, (a + dy) % NY) for a in range(NY)] for dy in range(NY)]
    blocks1, got1 = [items], [send1[0]]
    for dy in range(1, NY):
        blocks1.append(lax.ppermute(items, "y", along_y[dy]))
        got1.append(lax.ppermute(send1[dy], "y", along_y[dy]))
    got1, user_degree, cotangent = lax.optimization_barrier((got1, user_degree, cotangent))
    rows = user_degree.shape[0] // NX
    degrees = user_degree[:, None].astype(F32)
    degree = lax.dynamic_slice_in_dim(user_degree, x * rows, rows)[:, None].astype(F32)
    scaled_grad = (cotangent.astype(F32) / degrees).astype(BF16)
    near_grad = [scaled_grad] + [lax.ppermute(scaled_grad, "y", along_y[dy]) for dy in range(1, NY)]
    target = jnp.arange(NY * UGRP, dtype=jnp.int32)
    order3 = ((y - target // UGRP + NY) % NY) * UGRP + target % UGRP
    labels1 = jnp.concatenate([labels_of(part, cap1) for part in got1])
    bases1 = jnp.arange(NY, dtype=jnp.int32) * BLK
    got2 = all_to_all(send2, ("z", "c"))
    mine, other = products(labels1, bases1, got1, blocks1, zero, cap1, both1, both1 // NC, False)
    other = lax.ppermute(other, "c", [(0, 1), (1, 0)])
    part1 = (mine + other.astype(F32)).reshape(-1, F)
    got2, part1 = lax.optimization_barrier((got2, part1))
    summed = lax.psum_scatter(part1, "z", scatter_dimension=0, tiled=True)
    summed, near_grad, degree = lax.optimization_barrier((summed, near_grad, degree))
    bundle_emb = (summed / bundle_degree[:, None].astype(F32)).astype(BF16)
    mixed = jnp.dot(bundle_emb, weight, preferred_element_type=F32)
    activated = jax.nn.silu(mixed).astype(BF16)
    near_act = lax.all_gather(activated, ("z", "c"), axis=0, tiled=True)

    labels2 = labels_of(got2, cap2).reshape(-1)
    senders = jnp.arange(near2, dtype=jnp.int32)
    halves = ((senders + c) % NC) * (NZ * BLK) + (senders // NC) * BLK
    mine, other = products(
        labels2, halves, got2, near_grad, order3, cap2, NC * NZ * BLK, NZ * BLK, True
    )
    other = lax.ppermute(other, "c", [(0, 1), (1, 0)])
    both = (mine + other.astype(F32)).reshape(-1, F)
    near_act, both = lax.optimization_barrier((near_act, both))
    grad_act = lax.psum_scatter(both, "z", scatter_dimension=0, tiled=True)
    sigma = jax.nn.sigmoid(mixed)
    grad_mixed = (grad_act * sigma * (1.0 + mixed * (1.0 - sigma))).astype(BF16)
    local_grad = lax.dot_general(
        bundle_emb, grad_mixed, (((0,), (0,)), ((), ())), preferred_element_type=F32
    )
    grad_bundle = lax.dot_general(
        grad_mixed, weight, (((1,), (1,)), ((), ())), preferred_element_type=F32
    ).astype(BF16)

    part2 = products(
        labels2, senders * BLK, got2, [near_act], zero, cap2, NY * UGRP, 0, False
    )[0]
    got_part = all_to_all(part2.reshape(NY * NX, rows, F), ("y", "x"))
    gathered = jnp.sum(got_part.astype(F32), axis=0)
    user_part = (gathered / degree).astype(BF16)
    user_out = lax.all_gather(user_part, "x", axis=0, tiled=True)

    piece = jnp.sum(all_to_all(local_grad.reshape(near2, -1, F), ("z", "c")), axis=0)
    piece = jnp.sum(all_to_all(jnp.broadcast_to(piece, (NY * NX,) + piece.shape), ("y", "x")), axis=0)
    grad_weight = all_to_all(jnp.broadcast_to(piece, (near2,) + piece.shape), ("z", "c")).reshape(F, F)
    return (user_out, grad_weight, grad_bundle)


def solution(mesh):
    axes = Mesh(mesh.devices.reshape(NY, NZ, NC, NX), ALL)
    in_specs = (
        P(ALL, None),
        P(ALL, None, None),
        P(ALL),
        P(ALL, None),
        P(ALL),
        P(ALL, None, None),
        P(ALL),
        P(ALL, None),
        P(ALL),
        P(),
        P(ALL),
        P(WIDE),
        P(WIDE, None),
    )
    out_specs = (P(WIDE, None), P(), P(ALL, None))
    return jax.shard_map(local, mesh=axes, in_specs=in_specs, out_specs=out_specs, check_vma=False)
```

```python
import jax
import jax.numpy as jnp
from jax import lax
from jax.experimental import pallas as pl
from jax.experimental.pallas import tpu as pltpu
from jax.sharding import Mesh, PartitionSpec as P

F = 256
TILE = 128
TILES = 96
BLK = 4
UGRP = 16
NY, NZ, NC, NX = 4, 8, 2, 4
WIDE = ("y", "z", "c")
ALL = ("y", "z", "c", "x")
LAB = 16
BF16 = jnp.bfloat16
F32 = jnp.float32
VMEM_LIMIT = 48 * 1024 * 1024

SMEM_SPEC = pl.BlockSpec(memory_space=pltpu.SMEM)
VMEM_SPEC = pl.BlockSpec(memory_space=pltpu.VMEM)
ANY_SPEC = pl.BlockSpec(memory_space=pl.ANY)


def pack(indices, first, second):
    parts = (first, second)
    shapes = [(p["groups"], p["cap"] * TILE + LAB, TILE) for p in parts]

    def kernel(index_ref, *rest):
        groups1 = shapes[0][0]
        outs1, out2 = rest[2 : 2 + groups1], rest[2 + groups1]
        tiles1, tiles2, room1, room2, count, labels, in_sems, sems1, sem2 = rest[3 + groups1 :]
        loads = [
            pltpu.make_async_copy(rest[1], tiles2, in_sems.at[1]),
            pltpu.make_async_copy(rest[0], tiles1, in_sems.at[0]),
        ]
        for load in loads:
            load.start()
        own_y, own_c = index_ref[6 * TILES], index_ref[6 * TILES + 1]
        lane = lax.broadcasted_iota(jnp.int32, (1, TILE), 1)

        def lay(part, at, tiles_ref, room):
            groups, rows, _ = room.shape
            for g in range(groups):
                count[g] = 0
            labels[...] = jnp.full(labels.shape, float(BLK * part["dummy"]), F32)

            def step(t, carry):
                source, own, slot = (index_ref[at + i * TILES + t] for i in range(3))
                g = part["group_of"](own, own_y)
                rank = count[g]
                count[g] = rank + 1
                row = pl.multiple_of(rank * TILE, TILE)
                room[g, pl.ds(row, TILE), :] = tiles_ref[t]
                label = (BLK * part["block_of"](own, slot, own_c) + source).astype(F32)
                old = labels[pl.ds(g, 1), :]
                labels[pl.ds(g, 1), :] = jnp.where(lane == rank, label, old)
                return carry

            lax.fori_loop(0, TILES, step, 0)
            room[:, rows - LAB : rows, :] = jnp.broadcast_to(
                labels[0:groups][:, None, :], (groups, LAB, TILE)
            ).astype(BF16)

        loads[0].wait()
        lay(second, 3 * TILES, tiles2, room2)
        copies = [pltpu.make_async_copy(room2, out2, sem2)]
        copies[0].start()
        loads[1].wait()
        lay(first, 0, tiles1, room1)
        for g in range(groups1):
            copies.append(pltpu.make_async_copy(room1.at[g], outs1[g], sems1.at[g]))
            copies[-1].start()
        for copy in copies:
            copy.wait()

    out_shape = [jax.ShapeDtypeStruct(shapes[0][1:], BF16)] * shapes[0][0]
    out_shape.append(jax.ShapeDtypeStruct(shapes[1], BF16))
    most = max(shapes[0][0], shapes[1][0])
    outs = pl.pallas_call(
        kernel,
        out_shape=out_shape,
        in_specs=[SMEM_SPEC, ANY_SPEC, ANY_SPEC],
        out_specs=[ANY_SPEC] * len(out_shape),
        scratch_shapes=[
            pltpu.VMEM((TILES, TILE, TILE), BF16),
            pltpu.VMEM((TILES, TILE, TILE), BF16),
            pltpu.VMEM(shapes[0], BF16),
            pltpu.VMEM(shapes[1], BF16),
            pltpu.SMEM((most,), jnp.int32),
            pltpu.VMEM((most, TILE), F32),
            pltpu.SemaphoreType.DMA((2,)),
            pltpu.SemaphoreType.DMA((shapes[0][0],)),
            pltpu.SemaphoreType.DMA,
        ],
        compiler_params=pltpu.CompilerParams(vmem_limit_bytes=VMEM_LIMIT),
        cost_estimate=pl.CostEstimate(flops=0, bytes_accessed=16 * 1024 * 1024, transcendentals=0),
        name="pack",
    )(indices, first["tiles"], second["tiles"])
    return outs[:-1], outs[-1]


def labels_of(received, cap):
    return received[..., cap * TILE, :cap].astype(jnp.int32)


def products(labels, bases, received, blocks, order, cap, count, split_out, flip):
    many = isinstance(received, (list, tuple))
    tiles_in = list(received) if many else [received]
    groups = len(received) if many else received.shape[0]
    n_out = (split_out > 0) + (split_out < count)
    n_in, n_blocks = len(tiles_in), len(blocks)
    blocks = [b.reshape(-1, TILE, F) for b in blocks]
    starts = [sum(b.shape[0] for b in blocks[:i]) for i in range(len(blocks))]
    total = sum(b.shape[0] for b in blocks)

    def kernel(lab_ref, base_ref, order_ref, *rest):
        tile_refs, block_refs = rest[:n_in], rest[n_in : n_in + n_blocks]
        outs = rest[n_in + n_blocks : n_in + n_blocks + n_out]
        acc, room, tiles, sems, tile_sems = rest[n_in + n_blocks + n_out :]
        loads = [
            pltpu.make_async_copy(ref, room.at[pl.ds(starts[i], blocks[i].shape[0])], sems.at[i])
            for i, ref in enumerate(block_refs)
        ]
        rows = cap * TILE
        tile_loads = []
        for g in range(groups):
            source = tile_refs[g].at[pl.ds(0, rows), :] if many else tile_refs[0].at[g, pl.ds(0, rows), :]
            tile_loads.append(pltpu.make_async_copy(source, tiles.at[g], tile_sems.at[g]))
        for load in loads + tile_loads:
            load.start()
        acc[...] = jnp.zeros_like(acc)
        for load in loads:
            load.wait()

        def one(i, g, tile):
            lab = lab_ref[i]
            near = base_ref[g] + lax.rem(lab, BLK)
            far = lax.div(lab, BLK)
            if flip:
                empty = far >= total
                into = jnp.where(empty, count, near)
                block = room[order_ref[jnp.where(empty, 0, far)]]
                term = lax.dot_general(tile, block, (((0,), (0,)), ((), ())), preferred_element_type=F32)
            else:
                into = far
                term = jnp.dot(tile, room[near], preferred_element_type=F32)
            acc[into] = acc[into] + term

        for g in range(groups):

            def step(k, carry, g=g):
                row = pl.multiple_of(k * TILE, TILE)
                one(g * cap + k, g, tiles[g, pl.ds(row, TILE), :])
                return carry

            tile_loads[g].wait()
            lax.fori_loop(0, cap, step, 0, unroll=8)
        at = 0
        if split_out > 0:
            outs[at][...] = acc[0:split_out]
            at += 1
        if split_out < count:
            outs[at][...] = acc[split_out:count].astype(BF16)

    out_shape = []
    if split_out > 0:
        out_shape.append(jax.ShapeDtypeStruct((split_out, TILE, F), F32))
    if split_out < count:
        out_shape.append(jax.ShapeDtypeStruct((count - split_out, TILE, F), BF16))
    return pl.pallas_call(
        kernel,
        out_shape=out_shape,
        in_specs=[SMEM_SPEC, SMEM_SPEC, SMEM_SPEC] + [ANY_SPEC] * (n_in + n_blocks),
        out_specs=[VMEM_SPEC] * n_out,
        scratch_shapes=[
            pltpu.VMEM((count + 1, TILE, F), F32),
            pltpu.VMEM((total, TILE, F), BF16),
            pltpu.VMEM((groups, cap * TILE, TILE), BF16),
            pltpu.SemaphoreType.DMA((n_blocks,)),
            pltpu.SemaphoreType.DMA((groups,)),
        ],
        compiler_params=pltpu.CompilerParams(vmem_limit_bytes=VMEM_LIMIT),
        cost_estimate=pl.CostEstimate(
            flops=2 * groups * cap * TILE * TILE * F, bytes_accessed=12 * 1024 * 1024, transcendentals=0
        ),
        name="back_products" if flip else "products",
    )(labels, bases, order, *tiles_in, *blocks)


def all_to_all(value, axes):
    return lax.all_to_all(value, axes, split_axis=0, concat_axis=0, tiled=True)


def local(
    items,
    tile1_values,
    tile1_source,
    tile1_owner,
    tile1_slot,
    tile2_values,
    tile2_source,
    tile2_owner,
    tile2_slot,
    weight,
    bundle_degree,
    user_degree,
    cotangent,
):
    y, z, c, x = (lax.axis_index(a) for a in ALL)
    indices = jnp.concatenate(
        [
            tile1_source, tile1_owner[:, 0], tile1_slot,
            tile2_source, tile2_owner[:, 0], tile2_slot,
            jnp.stack([y, c]).astype(jnp.int32),
        ]
    )
    near1, near2 = NY, NZ * NC
    cap1, cap2 = TILE // near1, TILE // near2
    both1 = NC * NZ * BLK
    send1, send2 = pack(
        indices,
        dict(
            tiles=tile1_values,
            groups=near1, cap=cap1, dummy=both1,
            group_of=lambda own, own_y: (own // (NZ * NC) - own_y + NY) % NY,
            block_of=lambda own, slot, own_c: (((own + own_c) % NC) * NZ + (own // NC) % NZ) * BLK + slot,
        ),
        dict(
            tiles=tile2_values,
            groups=near2, cap=cap2, dummy=NY * UGRP,
            group_of=lambda own, own_y: own % (NZ * NC),
            block_of=lambda own, slot, own_c: (own // (NZ * NC)) * UGRP + slot,
        ),
    )
    zero = jnp.zeros((1,), jnp.int32)
    along_y = [[(a, (a + dy) % NY) for a in range(NY)] for dy in range(NY)]
    blocks1, got1 = [items], [send1[0]]
    for dy in range(1, NY):
        blocks1.append(lax.ppermute(items, "y", along_y[dy]))
        got1.append(lax.ppermute(send1[dy], "y", along_y[dy]))
    got1, user_degree, cotangent = lax.optimization_barrier((got1, user_degree, cotangent))
    rows = user_degree.shape[0] // NX
    degrees = user_degree[:, None].astype(F32)
    degree = lax.dynamic_slice_in_dim(user_degree, x * rows, rows)[:, None].astype(F32)
    scaled_grad = (cotangent.astype(F32) / degrees).astype(BF16)
    near_grad = [scaled_grad] + [lax.ppermute(scaled_grad, "y", along_y[dy]) for dy in range(1, NY)]
    target = jnp.arange(NY * UGRP, dtype=jnp.int32)
    order3 = ((y - target // UGRP + NY) % NY) * UGRP + target % UGRP
    labels1 = jnp.concatenate([labels_of(part, cap1) for part in got1])
    bases1 = jnp.arange(NY, dtype=jnp.int32) * BLK
    got2 = all_to_all(send2, ("z", "c"))
    mine, other = products(labels1, bases1, got1, blocks1, zero, cap1, both1, both1 // NC, False)
    other = lax.ppermute(other, "c", [(0, 1), (1, 0)])
    part1 = (mine + other.astype(F32)).reshape(-1, F)
    got2, part1 = lax.optimization_barrier((got2, part1))
    summed = lax.psum_scatter(part1, "z", scatter_dimension=0, tiled=True)
    summed, near_grad, degree = lax.optimization_barrier((summed, near_grad, degree))
    bundle_emb = (summed / bundle_degree[:, None].astype(F32)).astype(BF16)
    mixed = jnp.dot(bundle_emb, weight, preferred_element_type=F32)
    activated = jax.nn.silu(mixed).astype(BF16)
    near_act = lax.all_gather(activated, ("z", "c"), axis=0, tiled=True)

    labels2 = labels_of(got2, cap2).reshape(-1)
    senders = jnp.arange(near2, dtype=jnp.int32)
    halves = ((senders + c) % NC) * (NZ * BLK) + (senders // NC) * BLK
    mine, other = products(
        labels2, halves, got2, near_grad, order3, cap2, NC * NZ * BLK, NZ * BLK, True
    )
    other = lax.ppermute(other, "c", [(0, 1), (1, 0)])
    both = (mine + other.astype(F32)).reshape(-1, F)
    near_act, both = lax.optimization_barrier((near_act, both))
    grad_act = lax.psum_scatter(both, "z", scatter_dimension=0, tiled=True)
    sigma = jax.nn.sigmoid(mixed)
    grad_mixed = (grad_act * sigma * (1.0 + mixed * (1.0 - sigma))).astype(BF16)
    local_grad = lax.dot_general(
        bundle_emb, grad_mixed, (((0,), (0,)), ((), ())), preferred_element_type=F32
    )
    grad_bundle = lax.dot_general(
        grad_mixed, weight, (((1,), (1,)), ((), ())), preferred_element_type=F32
    ).astype(BF16)

    part2 = products(
        labels2, senders * BLK, got2, [near_act], zero, cap2, NY * UGRP, 0, False
    )[0]
    got_part = all_to_all(part2.reshape(NY * NX, rows, F), ("y", "x"))
    gathered = jnp.sum(got_part.astype(F32), axis=0)
    user_part = (gathered / degree).astype(BF16)
    user_out = lax.all_gather(user_part, "x", axis=0, tiled=True)

    piece = jnp.sum(all_to_all(local_grad.reshape(near2, -1, F), ("z", "c")), axis=0)
    piece = jnp.sum(all_to_all(jnp.broadcast_to(piece, (NY * NX,) + piece.shape), ("y", "x")), axis=0)
    grad_weight = all_to_all(jnp.broadcast_to(piece, (near2,) + piece.shape), ("z", "c")).reshape(F, F)
    return (user_out, grad_weight, grad_bundle)


def solution(mesh):
    axes = Mesh(mesh.devices.reshape(NY, NZ, NC, NX), ALL)
    in_specs = (
        P(ALL, None),
        P(ALL, None, None),
        P(ALL),
        P(ALL, None),
        P(ALL),
        P(ALL, None, None),
        P(ALL),
        P(ALL, None),
        P(ALL),
        P(),
        P(ALL),
        P(WIDE),
        P(WIDE, None),
    )
    out_specs = (P(WIDE, None), P(), P(ALL, None))
    return jax.shard_map(local, mesh=axes, in_specs=in_specs, out_specs=out_specs, check_vma=False)
```
